32 devices in a mesh: groups: 2 (over y), gx: 4 (over z), gy: 2 (over x), ta: 2 (over core).
Axes of the slice: x: 2, y: 2, z: 4, core: 2. Of those that a mesh axis runs over, the one named last changes fastest.
Arguments:
- frames: bfloat16 [4, 128, 16, 4, 512], P('gx', ('groups', 'ta'), None, 'gy'), parts along dimension 1, may hold values from -6 to 6
- start_state: float32 [128, 16, 4, 256], P(('groups', 'ta'), 'gx', 'gy'), parts along dimension 0, may hold values from -0.9 to 0.9
- tile_index: int32 [16, 4, 5], P('gx', 'gy'), may hold values from 0 to 7, as said below
- tile_bank: bfloat16 [8, 256, 256], replicated, may hold values from -1.25 to 1.25
- inlet_coupler: bfloat16 [512, 256], replicated, may hold values from -0.0546875 to 0.0546875
- readout_operator: bfloat16 [512, 512], replicated, may hold values from -0.25 to 0.25
Outputs:
- predicted_field: bfloat16 [128, 16, 4, 512], P(('groups', 'ta'), 'gx', 'gy'), parts along dimension 0
- final_state: float32 [128, 16, 4, 256], P(('groups', 'ta'), 'gx', 'gy'), parts along dimension 0
The draws below stay inside these ranges and needn't reach their ends.
There are 2 independent parts, one for each index of `groups`. The reference program is written for one: setup_inputs(seed, part) draws one part's arguments, and reference() takes and returns one part's arrays. A program takes and returns all parts, laid end to end along the dimension named above; an argument that names none is the same for every part. Nothing has to cross between parts.
Inputs may be any that keep to these rules, and one draw needn't show every extreme that they name: tile_index[x, y, 0], the tile that joins a block to itself, is below 4; the four neighbour entries are 4 or more.
All inputs are finite; a program needn't handle non-finite values.
Results may differ from the reference program's by a relative error of at most 0.0067.
Values may be sent and summed in bfloat16 or wider, within the bound.
No kernel may reach another device: no remote copies, remote signals or barrier semaphores. Data moves between devices by JAX's collectives and lax.ppermute only.
A program may use at most 64 MiB of HBM per device.

```python
import math
import jax
import jax.numpy as jnp
from jax import lax

UNITS = 256
PATCH = 512
NBANK = 8
STEPS = 4
NBX = 16
NBY = 4
TRAJ = 64


def draw_tile_index(key, part):
    key = jax.random.fold_in(key, 12)
    own_key, other_key = jax.random.split(key)
    half_bank = NBANK // 2
    own_tiles = jax.random.randint(own_key, (NBX, NBY, 1), 0, half_bank, dtype=jnp.int32)
    other_tiles = jax.random.randint(other_key, (NBX, NBY, 4), half_bank, NBANK, dtype=jnp.int32)
    return jnp.concatenate([own_tiles, other_tiles], axis=-1)


def draw_tile_bank(key, part):
    key = jax.random.fold_in(key, 11)
    noise_key, diag_key = jax.random.split(key)
    noise = jnp.clip(jax.random.normal(noise_key, (NBANK, UNITS, UNITS), jnp.float32), -4.0, 4.0)
    half_bank = NBANK // 2
    own_tiles = (jnp.arange(NBANK) < half_bank)[:, None, None]
    noise_scale = jnp.where(own_tiles, 0.3, 0.25) / math.sqrt(UNITS)
    diag_values = jax.random.uniform(diag_key, (NBANK, UNITS, 1), jnp.float32, 0.85, 0.99)
    identity_tile = (jnp.arange(UNITS)[:, None] == jnp.arange(UNITS)[None, :]).astype(jnp.float32)
    diagonal_part = jnp.where(own_tiles, diag_values * identity_tile[None, :, :], 0.0)
    return (diagonal_part + noise_scale * noise).astype(jnp.bfloat16)


def levels(rng, extent, cuts, least, high):
    loudness = 1.0
    for axis_at, shards_of in cuts:
        heights = jax.random.uniform(jax.random.fold_in(jax.random.fold_in(rng, 6), axis_at), (shards_of,), jnp.float32, least / len(cuts), high / len(cuts))
        loudness = loudness * jnp.repeat(jnp.exp(heights), extent[axis_at] // shards_of).reshape((-1,) + (1,) * (len(extent) - 1 - axis_at))
    return loudness


def scatter_about(stream_key, shape, scale, reach, shards=(), kind=jnp.bfloat16):
    drawn = jax.random.normal(stream_key, shape, jnp.float32) * scale
    if len(shards) > 0:
        drawn = levels(stream_key, shape, shards, -0.22, 0.18) * drawn
    return jnp.clip(drawn, min=-reach, max=reach).astype(kind)


def setup_inputs(seed: int = 0, part: int = 0) -> dict:
    seeds = jax.random.split(jax.random.key(seed), 7)
    part_keys = jax.random.split(jax.random.fold_in(seeds[6], part), 7)
    frames = scatter_about(part_keys[0], (STEPS, TRAJ, NBX, NBY, PATCH), 1.0, 6.0, ((0, 4), (1, 2), (3, 2)))
    start_state = jnp.clip(jax.random.uniform(part_keys[1], (TRAJ, NBX, NBY, UNITS), jnp.float32, -0.9, 0.9) * levels(part_keys[1], (TRAJ, NBX, NBY, UNITS), ((0, 2), (1, 4), (2, 2)), -0.4, 0.0), -0.9, 0.9)
    tile_index = draw_tile_index(jax.random.fold_in(seeds[6], 71), part)
    tile_bank = draw_tile_bank(jax.random.fold_in(seeds[6], 71), part)
    inlet_coupler = scatter_about(seeds[4], (PATCH, UNITS), (25 * PATCH) ** -0.5, 0.0546875)
    readout_operator = scatter_about(seeds[5], (2 * UNITS, PATCH), (2 * UNITS) ** -0.5, 0.25)
    return dict(frames=frames, start_state=start_state, tile_index=tile_index, tile_bank=tile_bank, inlet_coupler=inlet_coupler, readout_operator=readout_operator)


def couple(state_half, tile_index, tile_bank):
    adjacent_blocks = jnp.stack([state_half, jnp.roll(state_half, 1, 1), jnp.roll(state_half, -1, 1), jnp.roll(state_half, 1, 2), jnp.roll(state_half, -1, 2)], axis=0)

    def row_block(row_items):
        row_states, row_index = row_items
        selected_entries = tile_bank[row_index].astype(jnp.float32)
        return jnp.einsum("kcyu,ykuv->cyv", row_states.astype(jnp.float32), selected_entries)

    coupled = lax.map(row_block, (jnp.moveaxis(adjacent_blocks, 2, 0), tile_index))
    return jnp.moveaxis(coupled, 0, 1)


def reference(frames, start_state, tile_index, tile_bank, inlet_coupler, readout_operator):
    patch_site_total = inlet_coupler.shape[0]
    hidden_node_total = inlet_coupler.shape[1]
    echo_system = start_state
    for step_index in range(STEPS):
        logged_sample = frames[step_index]
        prediction_span = logged_sample.shape[:-1]
        input_signal = jnp.dot(logged_sample.reshape(-1, patch_site_total), inlet_coupler, preferred_element_type=jnp.float32).astype(jnp.bfloat16).reshape(prediction_span + (hidden_node_total,))
        state_half = echo_system.astype(jnp.bfloat16)
        coupled = couple(state_half, tile_index, tile_bank)
        echo_system = jnp.tanh(coupled + input_signal.astype(jnp.float32))
    readout_basis = jnp.concatenate([echo_system, echo_system * echo_system], axis=-1).astype(jnp.bfloat16)
    prediction_span = readout_basis.shape[:-1]
    predicted_field = jnp.dot(readout_basis.reshape(-1, 2 * hidden_node_total), readout_operator, preferred_element_type=jnp.float32).astype(jnp.bfloat16).reshape(prediction_span + (patch_site_total,))
    return predicted_field, echo_system
```

```python
import jax
import jax.numpy as jnp
from jax import lax
from jax.experimental import pallas as pl
from jax.experimental.pallas import tpu as pltpu
from jax.sharding import PartitionSpec as P

PLANE = ("gx", "gy")
VMEM_LIMIT = 40 * 1024 * 1024


def whole(shape):
    return pl.BlockSpec(shape, lambda *_: (0,) * len(shape))


def inlet_kernel(frames_ref, start_ref, inlet_ref, packed_ref):
    peers, rows, units = packed_ref.shape
    cells = frames_ref[...].reshape(-1, frames_ref.shape[-1])
    drive = jnp.dot(cells, inlet_ref[...], preferred_element_type=jnp.float32)
    drive_rows = drive.shape[0] // peers
    packed_ref[:, :drive_rows, :] = drive.astype(jnp.bfloat16).reshape(peers, drive_rows, units)
    state = start_ref[...].reshape(peers, rows - drive_rows, units)
    packed_ref[:, drive_rows:, :] = state.astype(jnp.bfloat16)


def pack_for_peers(frames, start_state, inlet_coupler, peers):
    units = inlet_coupler.shape[1]
    drive_rows = frames.size // frames.shape[-1] // peers
    state_rows = start_state.size // units // peers
    return pl.pallas_call(
        inlet_kernel,
        out_shape=jax.ShapeDtypeStruct((peers, drive_rows + state_rows, units), jnp.bfloat16),
        compiler_params=pltpu.CompilerParams(vmem_limit_bytes=VMEM_LIMIT),
    )(frames, start_state, inlet_coupler)


def steps_kernel(count_x, count_y, packed_ref, own_ref, from_ref, bank_ref, sent_ref):
    peers, rows, units = packed_ref.shape
    torus_rows = own_ref.shape[1]
    home_rows = torus_rows // count_x
    trajectories = sent_ref.shape[1] // home_rows
    drive_rows = trajectories * torus_rows
    halves = bank_ref.shape[0] // 2
    groups = [(j, t) for j in range(count_y) for t in range(trajectories)]

    def home_slice(t, base=0):
        return slice(base + t * home_rows, base + (t + 1) * home_rows)

    def choose(index, products):
        chosen = products[-1]
        for tile in range(halves - 2, -1, -1):
            chosen = jnp.where(index == tile, products[tile], chosen)
        return chosen

    column = lax.broadcasted_iota(jnp.int32, (torus_rows, units), 0) % 2
    low = column == 0
    state = []
    for j, t in groups:
        for i in range(count_x):
            piece = packed_ref[i * count_y + j, drive_rows : rows, :].astype(jnp.float32)
            state.append(piece[home_slice(t)])
    state = jnp.concatenate(state, axis=0)
    for step in range(count_x):
        state_half = state.astype(jnp.bfloat16)
        own = [
            jnp.dot(state_half, bank_ref[tile], preferred_element_type=jnp.float32)
            for tile in range(halves)
        ]
        other = [
            jnp.dot(state_half, bank_ref[halves + tile], preferred_element_type=jnp.float32)
            for tile in range(halves)
        ]
        kept, after_x, left, right = {}, {}, {}, {}
        for g, (j, t) in enumerate(groups):
            span = slice(g * torus_rows, (g + 1) * torus_rows)
            others = [product[span] for product in other]
            total = choose(own_ref[j], [product[span] for product in own])
            total += pltpu.roll(choose(from_ref[0, j], others), 2, axis=0)
            total += pltpu.roll(choose(from_ref[1, j], others), torus_rows - 2, axis=0)
            kept[j, t] = total
            left[j, t] = choose(from_ref[2, j], others)
            right[j, t] = choose(from_ref[3, j], others)
        fresh = []
        for j, t in groups:
            before, behind = (j - 1) % count_y, (j + 1) % count_y
            total = kept[j, t]
            total += jnp.where(
                low,
                pltpu.roll(left[before, t], torus_rows - 1, axis=0),
                pltpu.roll(left[j, t], 1, axis=0),
            )
            total += jnp.where(
                low,
                pltpu.roll(right[j, t], torus_rows - 1, axis=0),
                pltpu.roll(right[behind, t], 1, axis=0),
            )
            drive = packed_ref[
                step * count_y + j, t * torus_rows : (t + 1) * torus_rows, :
            ].astype(jnp.float32)
            fresh.append(jnp.tanh(total + drive))
        state = jnp.concatenate(fresh, axis=0)
    for i in range(count_x):
        for j in range(count_y):
            pieces = []
            for t in range(trajectories):
                base = (j * trajectories + t) * torus_rows + i * home_rows
                pieces.append(state[base : base + home_rows])
            sent_ref[i * count_y + j] = jnp.concatenate(pieces, axis=0).astype(jnp.bfloat16)


def run_steps(packed, own_index, from_index, tile_bank, count_x, count_y, home_rows):
    peers, _, units = packed.shape

    def kernel(*refs):
        steps_kernel(count_x, count_y, *refs)

    return pl.pallas_call(
        kernel,
        out_shape=jax.ShapeDtypeStruct((peers, home_rows, units), jnp.bfloat16),
        compiler_params=pltpu.CompilerParams(vmem_limit_bytes=VMEM_LIMIT),
    )(packed, own_index, from_index, tile_bank)


def readout_kernel(state_ref, readout_ref, field_ref, final_ref):
    units = state_ref.shape[-1]
    half = state_ref[...].reshape(-1, units)
    final = half.astype(jnp.float32)
    squares = (final * final).astype(jnp.bfloat16)
    field = jnp.dot(half, readout_ref[:units], preferred_element_type=jnp.float32)
    field += jnp.dot(squares, readout_ref[units:], preferred_element_type=jnp.float32)
    final_ref[...] = final.reshape(final_ref.shape)
    field_ref[...] = field.astype(jnp.bfloat16).reshape(field_ref.shape)


def read_out(state, readout_operator, block_shape):
    return pl.pallas_call(
        readout_kernel,
        out_shape=(
            jax.ShapeDtypeStruct(block_shape + readout_operator.shape[1:], jnp.bfloat16),
            jax.ShapeDtypeStruct(block_shape + state.shape[-1:], jnp.float32),
        ),
        compiler_params=pltpu.CompilerParams(vmem_limit_bytes=VMEM_LIMIT),
    )(state, readout_operator)


def tile_choices(tile_index, first_other, units):
    everywhere = lax.all_gather(tile_index, "gx", axis=0, tiled=True)
    everywhere = lax.all_gather(everywhere, "gy", axis=1, tiled=True)

    def by_row(index):
        pairs = index.reshape(index.shape[0], -1, 2).transpose(1, 0, 2)
        pairs = pairs.reshape(pairs.shape[0], -1, 1)
        return jnp.broadcast_to(pairs, pairs.shape[:2] + (units,))

    leaving = [
        jnp.roll(everywhere[..., 1], -1, 0),
        jnp.roll(everywhere[..., 2], 1, 0),
        jnp.roll(everywhere[..., 3], -1, 1),
        jnp.roll(everywhere[..., 4], 1, 1),
    ]
    return by_row(everywhere[..., 0]), jnp.stack([by_row(v) for v in leaving]) - first_other


def by_trajectory(frames, start_state, tile_index, tile_bank, inlet_coupler, readout_operator):
    count_x, count_y = lax.axis_size("gx"), lax.axis_size("gy")
    peers = count_x * count_y
    units = inlet_coupler.shape[1]
    block_shape = start_state.shape[:-1]
    packed = pack_for_peers(frames, start_state, inlet_coupler, peers)
    own_index, from_index = tile_choices(tile_index, tile_bank.shape[0] // 2, units)
    packed = lax.all_to_all(packed, PLANE, 0, 0, tiled=True)
    home_rows = start_state.size // units // peers
    sent = run_steps(packed, own_index, from_index, tile_bank, count_x, count_y, home_rows)
    state = lax.all_to_all(sent, PLANE, 0, 0, tiled=True)
    return read_out(state, readout_operator, block_shape)


def with_halo(cells, sides, width):
    for axis, dim in sides:
        count = lax.axis_size(axis)
        head = lax.slice_in_dim(cells, 0, width, axis=dim)
        tail = lax.slice_in_dim(cells, cells.shape[dim] - width, cells.shape[dim], axis=dim)
        cells = jnp.concatenate(
            [
                lax.ppermute(tail, axis, [(i, (i + 1) % count) for i in range(count)]),
                cells,
                lax.ppermute(head, axis, [((i + 1) % count, i) for i in range(count)]),
            ],
            axis=dim,
        )
    return cells


def by_block(frames, start_state, tile_index, tile_bank, inlet_coupler, readout_operator):
    patch_site_total = inlet_coupler.shape[0]
    hidden_node_total = inlet_coupler.shape[1]
    prediction_span = frames.shape[:-1]
    unrolled = jnp.dot(
        frames.reshape(-1, patch_site_total), inlet_coupler, preferred_element_type=jnp.float32
    )
    projected = unrolled.astype(jnp.bfloat16).reshape(prediction_span + (hidden_node_total,))
    input_signal = lax.all_to_all(projected, "gx", split_axis=2, concat_axis=0, tiled=True)
    chosen_tiles = tile_bank[tile_index]

    def advance(step_index, echo_system):
        state_half = echo_system.astype(jnp.bfloat16)
        extended = with_halo(state_half, (("gx", 1), ("gy", 2)), 1)
        adjacent_blocks = jnp.stack(
            [
                extended[:, 1:-1, 1:-1],
                extended[:, :-2, 1:-1],
                extended[:, 2:, 1:-1],
                extended[:, 1:-1, :-2],
                extended[:, 1:-1, 2:],
            ],
            axis=0,
        )
        coupled = jnp.einsum(
            "kcxyu,xykuv->cxyv", adjacent_blocks, chosen_tiles, preferred_element_type=jnp.float32
        )
        drive_now = lax.dynamic_index_in_dim(input_signal, step_index, 0, keepdims=False)
        return jnp.tanh(coupled + drive_now.astype(jnp.float32))

    echo_system = lax.fori_loop(0, input_signal.shape[0], advance, start_state)
    readout_basis = jnp.concatenate([echo_system, echo_system * echo_system], axis=-1).astype(
        jnp.bfloat16
    )
    prediction_span = readout_basis.shape[:-1]
    predicted_field = jnp.dot(
        readout_basis.reshape(-1, 2 * hidden_node_total),
        readout_operator,
        preferred_element_type=jnp.float32,
    )
    predicted_field = predicted_field.astype(jnp.bfloat16).reshape(
        prediction_span + (patch_site_total,)
    )
    return (predicted_field, echo_system)


def solution(mesh):
    placed = (
        P("gx", ("groups", "ta"), None, "gy", None),
        P(("groups", "ta"), "gx", "gy", None),
        P("gx", "gy", None),
        P(),
        P(),
        P(),
    )
    def shards(frames, start_state, *rest):
        peers = mesh.shape["gx"] * mesh.shape["gy"]
        fits = start_state.shape[0] % peers == 0 and start_state.shape[2] == 2
        fits = fits and start_state.shape[1] % 4 == 0
        body = by_trajectory if fits and frames.shape[0] == 1 else by_block
        return body(frames, start_state, *rest)

    return jax.shard_map(
        shards,
        mesh=mesh,
        in_specs=placed,
        out_specs=(P(("groups", "ta"), "gx", "gy", None), P(("groups", "ta"), "gx", "gy", None)),
        check_vma=False,
    )
```

```python
import jax
import jax.numpy as jnp
from jax import lax
from jax.experimental import pallas as pl
from jax.experimental.pallas import tpu as pltpu
from jax.sharding import PartitionSpec as P

PLANE = ("gx", "gy")
VMEM_LIMIT = 40 * 1024 * 1024
WIDE_VMEM_LIMIT = 60 * 1024 * 1024


def whole(shape):
    return pl.BlockSpec(shape, lambda *_: (0,) * len(shape))


def inlet_kernel(frames_ref, start_ref, index_ref, inlet_ref, packed_ref):
    peers, rows, units = packed_ref.shape
    entries = index_ref.shape[-1]
    cells = frames_ref[...].reshape(-1, frames_ref.shape[-1])
    drive = jnp.dot(cells, inlet_ref[...], preferred_element_type=jnp.float32)
    drive_rows = drive.shape[0] // peers
    packed_ref[:, :drive_rows, :] = drive.astype(jnp.bfloat16).reshape(peers, drive_rows, units)
    state_rows = start_ref.shape[0] * index_ref.shape[0] // peers
    state = start_ref[...].reshape(peers, state_rows, units)
    packed_ref[:, drive_rows : drive_rows + state_rows, :] = state.astype(jnp.bfloat16)
    index = jnp.broadcast_to(index_ref[...].astype(jnp.bfloat16)[None], (peers,) + index_ref.shape)
    packed_ref[:, drive_rows + state_rows :, :] = jnp.zeros((peers, index_ref.shape[0], units), jnp.bfloat16)
    packed_ref[:, drive_rows + state_rows :, :entries] = index


def pack_for_peers(frames, start_state, tile_index, inlet_coupler, peers):
    units = inlet_coupler.shape[1]
    blocks = tile_index.shape[0] * tile_index.shape[1]
    drive_rows = frames.size // frames.shape[-1] // peers
    state_rows = start_state.size // units // peers
    index = tile_index.reshape(blocks, -1)
    out_shape = (peers, drive_rows + state_rows + blocks, units)
    return pl.pallas_call(
        inlet_kernel,
        grid=(1,),
        in_specs=[whole(v.shape) for v in (frames, start_state, index, inlet_coupler)],
        out_specs=whole(out_shape),
        out_shape=jax.ShapeDtypeStruct(out_shape, jnp.bfloat16),
        compiler_params=pltpu.CompilerParams(vmem_limit_bytes=WIDE_VMEM_LIMIT),
    )(frames, start_state, index, inlet_coupler)


def neighbour_choices(packed_ref, base, count_x, count_y, first_other):
    units = packed_ref.shape[-1]

    def entry(j, k):
        parts = []
        for i in range(count_x):
            rows = packed_ref[i * count_y + j, base:, :].astype(jnp.float32)
            parts.append(jnp.broadcast_to(rows[:, k : k + 1], (rows.shape[0], units)))
        return jnp.concatenate(parts, axis=0)

    columns = range(count_y)
    own = [entry(j, 0) for j in columns]
    torus_rows = own[0].shape[0]
    low = lax.broadcasted_iota(jnp.int32, own[0].shape, 0) % 2 == 0
    left = [entry(j, 3) for j in columns]
    right = [entry(j, 4) for j in columns]
    other = []
    for j in columns:
        other.append(
            [
                pltpu.roll(entry(j, 1), torus_rows - 2, axis=0),
                pltpu.roll(entry(j, 2), 2, axis=0),
                jnp.where(
                    low,
                    pltpu.roll(left[j], torus_rows - 1, axis=0),
                    pltpu.roll(left[(j + 1) % count_y], 1, axis=0),
                ),
                jnp.where(
                    low,
                    pltpu.roll(right[j - 1], torus_rows - 1, axis=0),
                    pltpu.roll(right[j], 1, axis=0),
                ),
            ]
        )
    return own, [[v - first_other for v in choices] for choices in other], low


def steps_kernel(count_x, count_y, torus_rows, packed_ref, bank_ref, sent_ref):
    peers, rows, units = packed_ref.shape
    home_rows = torus_rows // count_x
    trajectories = sent_ref.shape[1] // home_rows
    drive_rows = trajectories * torus_rows
    state_rows = trajectories * home_rows
    halves = bank_ref.shape[0] // 2
    groups = [(j, t) for j in range(count_y) for t in range(trajectories)]

    def choose(index, products):
        chosen = products[-1]
        for tile in range(halves - 2, -1, -1):
            chosen = jnp.where(index == tile, products[tile], chosen)
        return chosen

    own_index, other_index, low = neighbour_choices(
        packed_ref, drive_rows + state_rows, count_x, count_y, halves
    )
    state = []
    for j, t in groups:
        for i in range(count_x):
            piece = packed_ref[i * count_y + j, drive_rows : drive_rows + state_rows, :]
            piece = piece.astype(jnp.float32)
            state.append(piece[t * home_rows : (t + 1) * home_rows])
    state = jnp.concatenate(state, axis=0)
    for step in range(count_x):
        state_half = state.astype(jnp.bfloat16)
        products = [
            jnp.dot(state_half, bank_ref[tile], preferred_element_type=jnp.float32)
            for tile in range(2 * halves)
        ]
        kept, left, right = {}, {}, {}
        for g, (j, t) in enumerate(groups):
            span = slice(g * torus_rows, (g + 1) * torus_rows)
            others = [product[span] for product in products[halves:]]
            total = choose(own_index[j], [product[span] for product in products[:halves]])
            total += pltpu.roll(choose(other_index[j][0], others), 2, axis=0)
            total += pltpu.roll(choose(other_index[j][1], others), torus_rows - 2, axis=0)
            kept[j, t] = total
            left[j, t] = choose(other_index[j][2], others)
            right[j, t] = choose(other_index[j][3], others)
        fresh = []
        for j, t in groups:
            before, behind = (j - 1) % count_y, (j + 1) % count_y
            total = kept[j, t]
            total += jnp.where(
                low,
                pltpu.roll(left[before, t], torus_rows - 1, axis=0),
                pltpu.roll(left[j, t], 1, axis=0),
            )
            total += jnp.where(
                low,
                pltpu.roll(right[j, t], torus_rows - 1, axis=0),
                pltpu.roll(right[behind, t], 1, axis=0),
            )
            drive = packed_ref[
                step * count_y + j, t * torus_rows : (t + 1) * torus_rows, :
            ].astype(jnp.float32)
            fresh.append(jnp.tanh(total + drive))
        state = jnp.concatenate(fresh, axis=0)
    for i in range(count_x):
        for j in range(count_y):
            pieces = []
            for t in range(trajectories):
                base = (j * trajectories + t) * torus_rows + i * home_rows
                pieces.append(state[base : base + home_rows])
            sent_ref[i * count_y + j] = jnp.concatenate(pieces, axis=0).astype(jnp.bfloat16)


def run_steps(packed, tile_bank, count_x, count_y, torus_rows, home_rows):
    peers, _, units = packed.shape

    def kernel(*refs):
        steps_kernel(count_x, count_y, torus_rows, *refs)

    return pl.pallas_call(
        kernel,
        out_shape=jax.ShapeDtypeStruct((peers, home_rows, units), jnp.bfloat16),
        compiler_params=pltpu.CompilerParams(vmem_limit_bytes=VMEM_LIMIT),
    )(packed, tile_bank)


def readout_kernel(state_ref, readout_ref, field_ref, final_ref):
    units = state_ref.shape[-1]
    half = state_ref[...].reshape(-1, units)
    final = half.astype(jnp.float32)
    squares = (final * final).astype(jnp.bfloat16)
    field = jnp.dot(half, readout_ref[:units], preferred_element_type=jnp.float32)
    field += jnp.dot(squares, readout_ref[units:], preferred_element_type=jnp.float32)
    final_ref[...] = final.reshape(final_ref.shape)
    field_ref[...] = field.astype(jnp.bfloat16).reshape(field_ref.shape)


def read_out(state, readout_operator, block_shape):
    return pl.pallas_call(
        readout_kernel,
        out_shape=(
            jax.ShapeDtypeStruct(block_shape + readout_operator.shape[1:], jnp.bfloat16),
            jax.ShapeDtypeStruct(block_shape + state.shape[-1:], jnp.float32),
        ),
        compiler_params=pltpu.CompilerParams(vmem_limit_bytes=VMEM_LIMIT),
    )(state, readout_operator)


def by_trajectory(frames, start_state, tile_index, tile_bank, inlet_coupler, readout_operator):
    count_x, count_y = lax.axis_size("gx"), lax.axis_size("gy")
    peers = count_x * count_y
    units = inlet_coupler.shape[1]
    block_shape = start_state.shape[:-1]
    packed = pack_for_peers(frames, start_state, tile_index, inlet_coupler, peers)
    packed = lax.all_to_all(packed, PLANE, 0, 0, tiled=True)
    torus_rows = frames.shape[2] * frames.shape[3]
    home_rows = start_state.size // units // peers
    sent = run_steps(packed, tile_bank, count_x, count_y, torus_rows, home_rows)
    state = lax.all_to_all(sent, PLANE, 0, 0, tiled=True)
    return read_out(state, readout_operator, block_shape)


def with_halo(cells, sides, width):
    for axis, dim in sides:
        count = lax.axis_size(axis)
        head = lax.slice_in_dim(cells, 0, width, axis=dim)
        tail = lax.slice_in_dim(cells, cells.shape[dim] - width, cells.shape[dim], axis=dim)
        cells = jnp.concatenate(
            [
                lax.ppermute(tail, axis, [(i, (i + 1) % count) for i in range(count)]),
                cells,
                lax.ppermute(head, axis, [((i + 1) % count, i) for i in range(count)]),
            ],
            axis=dim,
        )
    return cells


def by_block(frames, start_state, tile_index, tile_bank, inlet_coupler, readout_operator):
    patch_site_total = inlet_coupler.shape[0]
    hidden_node_total = inlet_coupler.shape[1]
    prediction_span = frames.shape[:-1]
    unrolled = jnp.dot(
        frames.reshape(-1, patch_site_total), inlet_coupler, preferred_element_type=jnp.float32
    )
    projected = unrolled.astype(jnp.bfloat16).reshape(prediction_span + (hidden_node_total,))
    input_signal = lax.all_to_all(projected, "gx", split_axis=2, concat_axis=0, tiled=True)
    chosen_tiles = tile_bank[tile_index]

    def advance(step_index, echo_system):
        state_half = echo_system.astype(jnp.bfloat16)
        extended = with_halo(state_half, (("gx", 1), ("gy", 2)), 1)
        adjacent_blocks = jnp.stack(
            [
                extended[:, 1:-1, 1:-1],
                extended[:, :-2, 1:-1],
                extended[:, 2:, 1:-1],
                extended[:, 1:-1, :-2],
                extended[:, 1:-1, 2:],
            ],
            axis=0,
        )
        coupled = jnp.einsum(
            "kcxyu,xykuv->cxyv", adjacent_blocks, chosen_tiles, preferred_element_type=jnp.float32
        )
        drive_now = lax.dynamic_index_in_dim(input_signal, step_index, 0, keepdims=False)
        return jnp.tanh(coupled + drive_now.astype(jnp.float32))

    echo_system = lax.fori_loop(0, input_signal.shape[0], advance, start_state)
    readout_basis = jnp.concatenate([echo_system, echo_system * echo_system], axis=-1).astype(
        jnp.bfloat16
    )
    prediction_span = readout_basis.shape[:-1]
    predicted_field = jnp.dot(
        readout_basis.reshape(-1, 2 * hidden_node_total),
        readout_operator,
        preferred_element_type=jnp.float32,
    )
    predicted_field = predicted_field.astype(jnp.bfloat16).reshape(
        prediction_span + (patch_site_total,)
    )
    return (predicted_field, echo_system)


def solution(mesh):
    placed = (
        P("gx", ("groups", "ta"), None, "gy", None),
        P(("groups", "ta"), "gx", "gy", None),
        P("gx", "gy", None),
        P(),
        P(),
        P(),
    )
    def shards(frames, start_state, *rest):
        peers = mesh.shape["gx"] * mesh.shape["gy"]
        fits = start_state.shape[0] % peers == 0 and start_state.shape[2] == 2
        fits = fits and start_state.shape[1] % 4 == 0
        body = by_trajectory if fits and frames.shape[0] == 1 else by_block
        return body(frames, start_state, *rest)

    return jax.shard_map(
        shards,
        mesh=mesh,
        in_specs=placed,
        out_specs=(P(("groups", "ta"), "gx", "gy", None), P(("groups", "ta"), "gx", "gy", None)),
        check_vma=False,
    )
```

```python
import jax
import jax.numpy as jnp
from jax import lax
from jax.experimental import pallas as pl
from jax.experimental.pallas import tpu as pltpu
from jax.sharding import PartitionSpec as P

PLANE = ("gx", "gy")
VMEM_LIMIT = 40 * 1024 * 1024
WIDE_VMEM_LIMIT = 60 * 1024 * 1024


def whole(shape):
    return pl.BlockSpec(shape, lambda *_: (0,) * len(shape))


def place_in_plane():
    return lax.axis_index("gx") * lax.axis_size("gy") + lax.axis_index("gy")


def place_in_plane():
    return lax.axis_index("gx") * lax.axis_size("gy") + lax.axis_index("gy")


def partners(peers):
    return list(range(peers - 1, -1, -1))


def inlet_kernel(peers, order, frames_hbm, start_hbm, index_ref, inlet_hbm, *refs):
    packed_refs, (frames_ref, start_ref, inlet_ref, arrived) = refs[:-4], refs[-4:]
    units = inlet_ref.shape[1]
    place = place_in_plane()
    share = frames_ref.shape[1]
    entries = index_ref.shape[-1]
    inlet_copy = pltpu.make_async_copy(inlet_hbm, inlet_ref, arrived.at[0, len(order)])
    inlet_copy.start()
    cell_copies, state_copies = [], []
    for slot, k in enumerate(order):
        mine = pl.ds((place ^ k) * share, share)
        cell_copies.append(
            pltpu.make_async_copy(frames_hbm.at[0, mine], frames_ref.at[slot], arrived.at[0, slot])
        )
        state_copies.append(
            pltpu.make_async_copy(start_hbm.at[mine], start_ref.at[slot], arrived.at[1, slot])
        )
    for copy in cell_copies + state_copies:
        copy.start()
    index = index_ref[...].astype(jnp.bfloat16)
    blank = jnp.zeros((index.shape[0], units), jnp.bfloat16)
    inlet_copy.wait()
    for slot, packed_ref in enumerate(packed_refs):
        cell_copies[slot].wait()
        cells = frames_ref[slot].reshape(-1, frames_ref.shape[-1])
        drive = jnp.dot(cells, inlet_ref[...], preferred_element_type=jnp.float32)
        drive_rows = drive.shape[0]
        packed_ref[:drive_rows, :] = drive.astype(jnp.bfloat16)
        state_copies[slot].wait()
        state = start_ref[slot].reshape(-1, units)
        after = drive_rows + state.shape[0]
        packed_ref[drive_rows:after, :] = state.astype(jnp.bfloat16)
        packed_ref[after:, :] = blank
        packed_ref[after:, :entries] = index


def pack_for_peers(frames, start_state, tile_index, inlet_coupler, peers, order, vmem_limit):
    units = inlet_coupler.shape[1]
    blocks = tile_index.shape[0] * tile_index.shape[1]
    drive_rows = frames.size // frames.shape[-1] // peers
    state_rows = start_state.size // units // peers
    index = tile_index.reshape(blocks, -1)
    out_shape = (drive_rows + state_rows + blocks, units)
    share = frames.shape[1] // peers
    far = pl.BlockSpec(memory_space=pltpu.HBM)

    def kernel(*refs):
        inlet_kernel(peers, order, *refs)

    return pl.pallas_call(
        kernel,
        in_specs=[far, far, pl.BlockSpec(memory_space=pltpu.VMEM), far],
        out_shape=[jax.ShapeDtypeStruct(out_shape, jnp.bfloat16)] * len(order),
        scratch_shapes=[
            pltpu.VMEM((len(order), share) + frames.shape[2:], frames.dtype),
            pltpu.VMEM((len(order), share) + start_state.shape[1:], start_state.dtype),
            pltpu.VMEM(inlet_coupler.shape, inlet_coupler.dtype),
            pltpu.SemaphoreType.DMA((2, len(order) + 1)),
        ],
        compiler_params=pltpu.CompilerParams(vmem_limit_bytes=vmem_limit),
    )(frames, start_state, index, inlet_coupler)


def exchange(frames, start_state, tile_index, inlet_coupler, peers):
    order = partners(peers)
    half = peers // 2
    got = []
    for part, limit in ((order[:half], WIDE_VMEM_LIMIT), (order[half:], VMEM_LIMIT)):
        packed = list(
            pack_for_peers(frames, start_state, tile_index, inlet_coupler, peers, part, limit)
        )
        tile_index, packed[0] = lax.optimization_barrier((tile_index, packed[0]))
        for k, block in zip(part, packed):
            if k:
                block = lax.ppermute(block, PLANE, [(p, p ^ k) for p in range(peers)])
            got.append(block)
    return got


def neighbour_choices(packed_ref, base, count_x, count_y, first_other):
    units = packed_ref.shape[-1]

    def entry(j, k):
        parts = []
        for i in range(count_x):
            rows = packed_ref[i * count_y + j, base:, :].astype(jnp.float32)
            parts.append(jnp.broadcast_to(rows[:, k : k + 1], (rows.shape[0], units)))
        return jnp.concatenate(parts, axis=0)

    columns = range(count_y)
    own = [entry(j, 0) for j in columns]
    torus_rows = own[0].shape[0]
    low = lax.broadcasted_iota(jnp.int32, own[0].shape, 0) % 2 == 0
    left = [entry(j, 3) for j in columns]
    right = [entry(j, 4) for j in columns]
    other = []
    for j in columns:
        other.append(
            [
                pltpu.roll(entry(j, 1), torus_rows - 2, axis=0),
                pltpu.roll(entry(j, 2), 2, axis=0),
                jnp.where(
                    low,
                    pltpu.roll(left[j], torus_rows - 1, axis=0),
                    pltpu.roll(left[(j + 1) % count_y], 1, axis=0),
                ),
                jnp.where(
                    low,
                    pltpu.roll(right[j - 1], torus_rows - 1, axis=0),
                    pltpu.roll(right[j], 1, axis=0),
                ),
            ]
        )
    return own, [[v - first_other for v in choices] for choices in other], low


def steps_kernel(count_x, count_y, torus_rows, *refs):
    got_refs, (bank_ref, sent_ref, packed_ref) = refs[:-3], refs[-3:]
    peers, rows, units = packed_ref.shape
    place = place_in_plane()
    for k, got_ref in zip(partners(peers), got_refs):
        packed_ref[place ^ k] = got_ref[...]
    home_rows = torus_rows // count_x
    trajectories = sent_ref.shape[1] // home_rows
    drive_rows = trajectories * torus_rows
    state_rows = trajectories * home_rows
    halves = bank_ref.shape[0] // 2
    groups = [(j, t) for j in range(count_y) for t in range(trajectories)]

    def choose(index, products):
        chosen = products[-1]
        for tile in range(halves - 2, -1, -1):
            chosen = jnp.where(index == tile, products[tile], chosen)
        return chosen

    own_index, other_index, low = neighbour_choices(
        packed_ref, drive_rows + state_rows, count_x, count_y, halves
    )
    state = []
    for j, t in groups:
        for i in range(count_x):
            piece = packed_ref[i * count_y + j, drive_rows : drive_rows + state_rows, :]
            piece = piece.astype(jnp.float32)
            state.append(piece[t * home_rows : (t + 1) * home_rows])
    state = jnp.concatenate(state, axis=0)
    for step in range(count_x):
        state_half = state.astype(jnp.bfloat16)
        products = [
            jnp.dot(state_half, bank_ref[tile], preferred_element_type=jnp.float32)
            for tile in range(2 * halves)
        ]
        kept, left, right = {}, {}, {}
        for g, (j, t) in enumerate(groups):
            span = slice(g * torus_rows, (g + 1) * torus_rows)
            others = [product[span] for product in products[halves:]]
            total = choose(own_index[j], [product[span] for product in products[:halves]])
            total += pltpu.roll(choose(other_index[j][0], others), 2, axis=0)
            total += pltpu.roll(choose(other_index[j][1], others), torus_rows - 2, axis=0)
            kept[j, t] = total
            left[j, t] = choose(other_index[j][2], others)
            right[j, t] = choose(other_index[j][3], others)
        fresh = []
        for j, t in groups:
            before, behind = (j - 1) % count_y, (j + 1) % count_y
            total = kept[j, t]
            total += jnp.where(
                low,
                pltpu.roll(left[before, t], torus_rows - 1, axis=0),
                pltpu.roll(left[j, t], 1, axis=0),
            )
            total += jnp.where(
                low,
                pltpu.roll(right[j, t], torus_rows - 1, axis=0),
                pltpu.roll(right[behind, t], 1, axis=0),
            )
            drive = packed_ref[
                step * count_y + j, t * torus_rows : (t + 1) * torus_rows, :
            ].astype(jnp.float32)
            fresh.append(jnp.tanh(total + drive))
        state = jnp.concatenate(fresh, axis=0)
    for i in range(count_x):
        for j in range(count_y):
            pieces = []
            for t in range(trajectories):
                base = (j * trajectories + t) * torus_rows + i * home_rows
                pieces.append(state[base : base + home_rows])
            sent_ref[i * count_y + j] = jnp.concatenate(pieces, axis=0).astype(jnp.bfloat16)


def run_steps(packed, tile_bank, count_x, count_y, torus_rows, home_rows):
    peers = len(packed)
    rows, units = packed[0].shape

    def kernel(*refs):
        steps_kernel(count_x, count_y, torus_rows, *refs)

    return pl.pallas_call(
        kernel,
        out_shape=jax.ShapeDtypeStruct((peers, home_rows, units), jnp.bfloat16),
        scratch_shapes=[pltpu.VMEM((peers, rows, units), jnp.bfloat16)],
        compiler_params=pltpu.CompilerParams(vmem_limit_bytes=VMEM_LIMIT),
    )(*packed, tile_bank)


def readout_kernel(state_ref, readout_ref, field_ref, final_ref):
    units = state_ref.shape[-1]
    half = state_ref[...].reshape(-1, units)
    final = half.astype(jnp.float32)
    squares = (final * final).astype(jnp.bfloat16)
    field = jnp.dot(half, readout_ref[:units], preferred_element_type=jnp.float32)
    field += jnp.dot(squares, readout_ref[units:], preferred_element_type=jnp.float32)
    final_ref[...] = final.reshape(final_ref.shape)
    field_ref[...] = field.astype(jnp.bfloat16).reshape(field_ref.shape)


def read_out(state, readout_operator, block_shape):
    return pl.pallas_call(
        readout_kernel,
        out_shape=(
            jax.ShapeDtypeStruct(block_shape + readout_operator.shape[1:], jnp.bfloat16),
            jax.ShapeDtypeStruct(block_shape + state.shape[-1:], jnp.float32),
        ),
        compiler_params=pltpu.CompilerParams(vmem_limit_bytes=VMEM_LIMIT),
    )(state, readout_operator)


def by_trajectory(frames, start_state, tile_index, tile_bank, inlet_coupler, readout_operator):
    count_x, count_y = lax.axis_size("gx"), lax.axis_size("gy")
    peers = count_x * count_y
    units = inlet_coupler.shape[1]
    block_shape = start_state.shape[:-1]
    packed = exchange(frames, start_state, tile_index, inlet_coupler, peers)
    torus_rows = frames.shape[2] * frames.shape[3]
    home_rows = start_state.size // units // peers
    sent = run_steps(packed, tile_bank, count_x, count_y, torus_rows, home_rows)
    state = lax.all_to_all(sent, PLANE, 0, 0, tiled=True)
    return read_out(state, readout_operator, block_shape)


def with_halo(cells, sides, width):
    for axis, dim in sides:
        count = lax.axis_size(axis)
        head = lax.slice_in_dim(cells, 0, width, axis=dim)
        tail = lax.slice_in_dim(cells, cells.shape[dim] - width, cells.shape[dim], axis=dim)
        cells = jnp.concatenate(
            [
                lax.ppermute(tail, axis, [(i, (i + 1) % count) for i in range(count)]),
                cells,
                lax.ppermute(head, axis, [((i + 1) % count, i) for i in range(count)]),
            ],
            axis=dim,
        )
    return cells


def by_block(frames, start_state, tile_index, tile_bank, inlet_coupler, readout_operator):
    patch_site_total = inlet_coupler.shape[0]
    hidden_node_total = inlet_coupler.shape[1]
    prediction_span = frames.shape[:-1]
    unrolled = jnp.dot(
        frames.reshape(-1, patch_site_total), inlet_coupler, preferred_element_type=jnp.float32
    )
    projected = unrolled.astype(jnp.bfloat16).reshape(prediction_span + (hidden_node_total,))
    input_signal = lax.all_to_all(projected, "gx", split_axis=2, concat_axis=0, tiled=True)
    chosen_tiles = tile_bank[tile_index]

    def advance(step_index, echo_system):
        state_half = echo_system.astype(jnp.bfloat16)
        extended = with_halo(state_half, (("gx", 1), ("gy", 2)), 1)
        adjacent_blocks = jnp.stack(
            [
                extended[:, 1:-1, 1:-1],
                extended[:, :-2, 1:-1],
                extended[:, 2:, 1:-1],
                extended[:, 1:-1, :-2],
                extended[:, 1:-1, 2:],
            ],
            axis=0,
        )
        coupled = jnp.einsum(
            "kcxyu,xykuv->cxyv", adjacent_blocks, chosen_tiles, preferred_element_type=jnp.float32
        )
        drive_now = lax.dynamic_index_in_dim(input_signal, step_index, 0, keepdims=False)
        return jnp.tanh(coupled + drive_now.astype(jnp.float32))

    echo_system = lax.fori_loop(0, input_signal.shape[0], advance, start_state)
    readout_basis = jnp.concatenate([echo_system, echo_system * echo_system], axis=-1).astype(
        jnp.bfloat16
    )
    prediction_span = readout_basis.shape[:-1]
    predicted_field = jnp.dot(
        readout_basis.reshape(-1, 2 * hidden_node_total),
        readout_operator,
        preferred_element_type=jnp.float32,
    )
    predicted_field = predicted_field.astype(jnp.bfloat16).reshape(
        prediction_span + (patch_site_total,)
    )
    return (predicted_field, echo_system)


def solution(mesh):
    placed = (
        P("gx", ("groups", "ta"), None, "gy", None),
        P(("groups", "ta"), "gx", "gy", None),
        P("gx", "gy", None),
        P(),
        P(),
        P(),
    )
    def shards(frames, start_state, *rest):
        peers = mesh.shape["gx"] * mesh.shape["gy"]
        fits = start_state.shape[0] % peers == 0 and peers & (peers - 1) == 0 and start_state.shape[2] == 2
        fits = fits and start_state.shape[1] % 4 == 0
        body = by_trajectory if fits and frames.shape[0] == 1 else by_block
        return body(frames, start_state, *rest)

    return jax.shard_map(
        shards,
        mesh=mesh,
        in_specs=placed,
        out_specs=(P(("groups", "ta"), "gx", "gy", None), P(("groups", "ta"), "gx", "gy", None)),
        check_vma=False,
    )
```

```python
import jax
import jax.numpy as jnp
from jax import lax
from jax.experimental import pallas as pl
from jax.experimental.pallas import tpu as pltpu
from jax.sharding import PartitionSpec as P

PLANE = ("gx", "gy")
VMEM_LIMIT = 24 * 1024 * 1024


def whole(shape):
    return pl.BlockSpec(shape, lambda *_: (0,) * len(shape))


def place_in_plane():
    return lax.axis_index("gx") * lax.axis_size("gy") + lax.axis_index("gy")


def place_in_plane():
    return lax.axis_index("gx") * lax.axis_size("gy") + lax.axis_index("gy")


def partners(peers):
    return sorted(range(peers), key=lambda k: (-k.bit_count(), -k))


def inlet_kernel(order, frames_hbm, start_hbm, index_hbm, inlet_hbm, *refs):
    count = len(order)
    packed_refs, (frames_ref, start_ref, index_ref, inlet_ref, arrived) = refs[:count], refs[count:]
    units = inlet_ref.shape[1]
    place = place_in_plane()
    share = frames_ref.shape[1]
    entries = index_ref.shape[-1]
    cell_copies, state_copies = [], []
    for slot, k in enumerate(order):
        mine = pl.ds((place ^ k) * share, share)
        cell_copies.append(
            pltpu.make_async_copy(frames_hbm.at[0, mine], frames_ref.at[slot], arrived.at[0, slot])
        )
        state_copies.append(
            pltpu.make_async_copy(start_hbm.at[mine], start_ref.at[slot], arrived.at[1, slot])
        )
    inlet_copy = pltpu.make_async_copy(inlet_hbm, inlet_ref, arrived.at[0, count])
    index_copy = pltpu.make_async_copy(index_hbm, index_ref, arrived.at[1, count])
    inlet_copy.start()
    for copy in cell_copies:
        copy.start()
    index_copy.start()
    for copy in state_copies:
        copy.start()
    inlet_copy.wait()
    for slot, packed_ref in enumerate(packed_refs):
        cell_copies[slot].wait()
        cells = frames_ref[slot].reshape(-1, frames_ref.shape[-1])
        drive = jnp.dot(cells, inlet_ref[...], preferred_element_type=jnp.float32)
        drive_rows = drive.shape[0]
        packed_ref[:drive_rows, :] = drive.astype(jnp.bfloat16)
        if slot == 0:
            index_copy.wait()
            index = index_ref[...].astype(jnp.bfloat16)
            blank = jnp.zeros((index.shape[0], units), jnp.bfloat16)
        state_copies[slot].wait()
        state = start_ref[slot].reshape(-1, units)
        after = drive_rows + state.shape[0]
        packed_ref[drive_rows:after, :] = state.astype(jnp.bfloat16)
        packed_ref[after:, :] = blank
        packed_ref[after:, :entries] = index


def pack_for_peers(frames, start_state, tile_index, inlet_coupler, peers, order):
    units = inlet_coupler.shape[1]
    blocks = tile_index.shape[0] * tile_index.shape[1]
    drive_rows = frames.size // frames.shape[-1] // peers
    state_rows = start_state.size // units // peers
    index = tile_index.reshape(blocks, -1)
    out_shape = (drive_rows + state_rows + blocks, units)
    share = frames.shape[1] // peers
    count = len(order)
    operands = [
        pltpu.with_memory_space_constraint(v, pltpu.HBM)
        for v in (frames, start_state, index, inlet_coupler)
    ]

    def kernel(*refs):
        inlet_kernel(order, *refs)

    return pl.pallas_call(
        kernel,
        in_specs=[pl.BlockSpec(memory_space=pltpu.HBM)] * len(operands),
        out_specs=[pl.BlockSpec(memory_space=pltpu.VMEM)] * count,
        out_shape=[pltpu.VMEM(out_shape, jnp.bfloat16)] * count,
        scratch_shapes=[
            pltpu.VMEM((count, share) + frames.shape[2:], frames.dtype),
            pltpu.VMEM((count, share) + start_state.shape[1:], start_state.dtype),
            pltpu.VMEM(index.shape, index.dtype),
            pltpu.VMEM(inlet_coupler.shape, inlet_coupler.dtype),
            pltpu.SemaphoreType.DMA((2, count + 1)),
        ],
        compiler_params=pltpu.CompilerParams(vmem_limit_bytes=VMEM_LIMIT),
    )(*operands)


def exchange(frames, start_state, tile_index, inlet_coupler, peers):
    order = partners(peers)
    first = 1
    got = []
    for part in (order[:first], order[first:]):
        packed = list(pack_for_peers(frames, start_state, tile_index, inlet_coupler, peers, part))
        tile_index, packed[0] = lax.optimization_barrier((tile_index, packed[0]))
        for k, block in zip(part, packed):
            if k:
                block = lax.ppermute(block, PLANE, [(p, p ^ k) for p in range(peers)])
            got.append(block)
    return got


def neighbour_choices(packed_ref, base, count_x, count_y, first_other):
    units = packed_ref.shape[-1]

    def entry(j, k):
        parts = []
        for i in range(count_x):
            rows = packed_ref[i * count_y + j, base:, :].astype(jnp.float32)
            parts.append(jnp.broadcast_to(rows[:, k : k + 1], (rows.shape[0], units)))
        return jnp.concatenate(parts, axis=0)

    columns = range(count_y)
    own = [entry(j, 0) for j in columns]
    torus_rows = own[0].shape[0]
    low = lax.broadcasted_iota(jnp.int32, own[0].shape, 0) % 2 == 0
    left = [entry(j, 3) for j in columns]
    right = [entry(j, 4) for j in columns]
    other = []
    for j in columns:
        other.append(
            [
                pltpu.roll(entry(j, 1), torus_rows - 2, axis=0),
                pltpu.roll(entry(j, 2), 2, axis=0),
                jnp.where(
                    low,
                    pltpu.roll(left[j], torus_rows - 1, axis=0),
                    pltpu.roll(left[(j + 1) % count_y], 1, axis=0),
                ),
                jnp.where(
                    low,
                    pltpu.roll(right[j - 1], torus_rows - 1, axis=0),
                    pltpu.roll(right[j], 1, axis=0),
                ),
            ]
        )
    return own, [[v - first_other for v in choices] for choices in other], low


def steps_kernel(count_x, count_y, torus_rows, *refs):
    got_refs, (bank_ref, sent_ref, packed_ref) = refs[:-3], refs[-3:]
    peers, rows, units = packed_ref.shape
    place = place_in_plane()
    for k, got_ref in zip(partners(peers), got_refs):
        packed_ref[place ^ k] = got_ref[...]
    home_rows = torus_rows // count_x
    trajectories = sent_ref.shape[1] // home_rows
    drive_rows = trajectories * torus_rows
    state_rows = trajectories * home_rows
    halves = bank_ref.shape[0] // 2
    groups = [(j, t) for j in range(count_y) for t in range(trajectories)]

    def choose(index, products):
        chosen = products[-1]
        for tile in range(halves - 2, -1, -1):
            chosen = jnp.where(index == tile, products[tile], chosen)
        return chosen

    own_index, other_index, low = neighbour_choices(
        packed_ref, drive_rows + state_rows, count_x, count_y, halves
    )
    state = []
    for j, t in groups:
        for i in range(count_x):
            piece = packed_ref[i * count_y + j, drive_rows : drive_rows + state_rows, :]
            piece = piece.astype(jnp.float32)
            state.append(piece[t * home_rows : (t + 1) * home_rows])
    state = jnp.concatenate(state, axis=0)
    for step in range(count_x):
        state_half = state.astype(jnp.bfloat16)
        products = [
            jnp.dot(state_half, bank_ref[tile], preferred_element_type=jnp.float32)
            for tile in range(2 * halves)
        ]
        kept, left, right = {}, {}, {}
        for g, (j, t) in enumerate(groups):
            span = slice(g * torus_rows, (g + 1) * torus_rows)
            others = [product[span] for product in products[halves:]]
            total = choose(own_index[j], [product[span] for product in products[:halves]])
            total += pltpu.roll(choose(other_index[j][0], others), 2, axis=0)
            total += pltpu.roll(choose(other_index[j][1], others), torus_rows - 2, axis=0)
            kept[j, t] = total
            left[j, t] = choose(other_index[j][2], others)
            right[j, t] = choose(other_index[j][3], others)
        fresh = []
        for j, t in groups:
            before, behind = (j - 1) % count_y, (j + 1) % count_y
            total = kept[j, t]
            total += jnp.where(
                low,
                pltpu.roll(left[before, t], torus_rows - 1, axis=0),
                pltpu.roll(left[j, t], 1, axis=0),
            )
            total += jnp.where(
                low,
                pltpu.roll(right[j, t], torus_rows - 1, axis=0),
                pltpu.roll(right[behind, t], 1, axis=0),
            )
            drive = packed_ref[
                step * count_y + j, t * torus_rows : (t + 1) * torus_rows, :
            ].astype(jnp.float32)
            fresh.append(jnp.tanh(total + drive))
        state = jnp.concatenate(fresh, axis=0)
    for i in range(count_x):
        for j in range(count_y):
            pieces = []
            for t in range(trajectories):
                base = (j * trajectories + t) * torus_rows + i * home_rows
                pieces.append(state[base : base + home_rows])
            sent_ref[i * count_y + j] = jnp.concatenate(pieces, axis=0).astype(jnp.bfloat16)


def run_steps(packed, tile_bank, count_x, count_y, torus_rows, home_rows):
    peers = len(packed)
    rows, units = packed[0].shape

    def kernel(*refs):
        steps_kernel(count_x, count_y, torus_rows, *refs)

    return pl.pallas_call(
        kernel,
        out_shape=jax.ShapeDtypeStruct((peers, home_rows, units), jnp.bfloat16),
        scratch_shapes=[pltpu.VMEM((peers, rows, units), jnp.bfloat16)],
        compiler_params=pltpu.CompilerParams(vmem_limit_bytes=VMEM_LIMIT),
    )(*packed, tile_bank)


def readout_kernel(state_ref, readout_ref, field_ref, final_ref):
    units = state_ref.shape[-1]
    half = state_ref[...].reshape(-1, units)
    final = half.astype(jnp.float32)
    squares = (final * final).astype(jnp.bfloat16)
    field = jnp.dot(half, readout_ref[:units], preferred_element_type=jnp.float32)
    field += jnp.dot(squares, readout_ref[units:], preferred_element_type=jnp.float32)
    final_ref[...] = final.reshape(final_ref.shape)
    field_ref[...] = field.astype(jnp.bfloat16).reshape(field_ref.shape)


def read_out(state, readout_operator, block_shape):
    return pl.pallas_call(
        readout_kernel,
        out_shape=(
            jax.ShapeDtypeStruct(block_shape + readout_operator.shape[1:], jnp.bfloat16),
            jax.ShapeDtypeStruct(block_shape + state.shape[-1:], jnp.float32),
        ),
        compiler_params=pltpu.CompilerParams(vmem_limit_bytes=VMEM_LIMIT),
    )(state, readout_operator)


def by_trajectory(frames, start_state, tile_index, tile_bank, inlet_coupler, readout_operator):
    count_x, count_y = lax.axis_size("gx"), lax.axis_size("gy")
    peers = count_x * count_y
    units = inlet_coupler.shape[1]
    block_shape = start_state.shape[:-1]
    packed = exchange(frames, start_state, tile_index, inlet_coupler, peers)
    torus_rows = frames.shape[2] * frames.shape[3]
    home_rows = start_state.size // units // peers
    sent = run_steps(packed, tile_bank, count_x, count_y, torus_rows, home_rows)
    state = lax.all_to_all(sent, PLANE, 0, 0, tiled=True)
    return read_out(state, readout_operator, block_shape)


def with_halo(cells, sides, width):
    for axis, dim in sides:
        count = lax.axis_size(axis)
        head = lax.slice_in_dim(cells, 0, width, axis=dim)
        tail = lax.slice_in_dim(cells, cells.shape[dim] - width, cells.shape[dim], axis=dim)
        cells = jnp.concatenate(
            [
                lax.ppermute(tail, axis, [(i, (i + 1) % count) for i in range(count)]),
                cells,
                lax.ppermute(head, axis, [((i + 1) % count, i) for i in range(count)]),
            ],
            axis=dim,
        )
    return cells


def by_block(frames, start_state, tile_index, tile_bank, inlet_coupler, readout_operator):
    patch_site_total = inlet_coupler.shape[0]
    hidden_node_total = inlet_coupler.shape[1]
    prediction_span = frames.shape[:-1]
    unrolled = jnp.dot(
        frames.reshape(-1, patch_site_total), inlet_coupler, preferred_element_type=jnp.float32
    )
    projected = unrolled.astype(jnp.bfloat16).reshape(prediction_span + (hidden_node_total,))
    input_signal = lax.all_to_all(projected, "gx", split_axis=2, concat_axis=0, tiled=True)
    chosen_tiles = tile_bank[tile_index]

    def advance(step_index, echo_system):
        state_half = echo_system.astype(jnp.bfloat16)
        extended = with_halo(state_half, (("gx", 1), ("gy", 2)), 1)
        adjacent_blocks = jnp.stack(
            [
                extended[:, 1:-1, 1:-1],
                extended[:, :-2, 1:-1],
                extended[:, 2:, 1:-1],
                extended[:, 1:-1, :-2],
                extended[:, 1:-1, 2:],
            ],
            axis=0,
        )
        coupled = jnp.einsum(
            "kcxyu,xykuv->cxyv", adjacent_blocks, chosen_tiles, preferred_element_type=jnp.float32
        )
        drive_now = lax.dynamic_index_in_dim(input_signal, step_index, 0, keepdims=False)
        return jnp.tanh(coupled + drive_now.astype(jnp.float32))

    echo_system = lax.fori_loop(0, input_signal.shape[0], advance, start_state)
    readout_basis = jnp.concatenate([echo_system, echo_system * echo_system], axis=-1).astype(
        jnp.bfloat16
    )
    prediction_span = readout_basis.shape[:-1]
    predicted_field = jnp.dot(
        readout_basis.reshape(-1, 2 * hidden_node_total),
        readout_operator,
        preferred_element_type=jnp.float32,
    )
    predicted_field = predicted_field.astype(jnp.bfloat16).reshape(
        prediction_span + (patch_site_total,)
    )
    return (predicted_field, echo_system)


def solution(mesh):
    placed = (
        P("gx", ("groups", "ta"), None, "gy", None),
        P(("groups", "ta"), "gx", "gy", None),
        P("gx", "gy", None),
        P(),
        P(),
        P(),
    )
    def shards(frames, start_state, *rest):
        peers = mesh.shape["gx"] * mesh.shape["gy"]
        fits = start_state.shape[0] % peers == 0 and peers & (peers - 1) == 0 and start_state.shape[2] == 2
        fits = fits and start_state.shape[1] % 4 == 0
        body = by_trajectory if fits and frames.shape[0] == 1 else by_block
        return body(frames, start_state, *rest)

    return jax.shard_map(
        shards,
        mesh=mesh,
        in_specs=placed,
        out_specs=(P(("groups", "ta"), "gx", "gy", None), P(("groups", "ta"), "gx", "gy", None)),
        check_vma=False,
    )
```

```python
import jax
import jax.numpy as jnp
from jax import lax
from jax.experimental import pallas as pl
from jax.experimental.pallas import tpu as pltpu
from jax.sharding import PartitionSpec as P

PLANE = ("gx", "gy")
VMEM_LIMIT = 24 * 1024 * 1024


def whole(shape):
    return pl.BlockSpec(shape, lambda *_: (0,) * len(shape))


def place_in_plane():
    return lax.axis_index("gx") * lax.axis_size("gy") + lax.axis_index("gy")


def place_in_plane():
    return lax.axis_index("gx") * lax.axis_size("gy") + lax.axis_index("gy")


def partners(peers):
    return sorted(range(peers), key=lambda k: (-k.bit_count(), -k))


def inlet_kernel(order, frames_hbm, start_hbm, index_hbm, inlet_hbm, *refs):
    count = len(order)
    packed_refs, (frames_ref, start_ref, index_ref, inlet_ref, arrived) = refs[:count], refs[count:]
    units = inlet_ref.shape[1]
    place = place_in_plane()
    share = frames_ref.shape[1]
    entries = index_ref.shape[-1]
    cell_copies, state_copies = [], []
    for slot, k in enumerate(order):
        mine = pl.ds((place ^ k) * share, share)
        cell_copies.append(
            pltpu.make_async_copy(frames_hbm.at[0, mine], frames_ref.at[slot], arrived.at[0, slot])
        )
        state_copies.append(
            pltpu.make_async_copy(start_hbm.at[mine], start_ref.at[slot], arrived.at[1, slot])
        )
    inlet_copy = pltpu.make_async_copy(inlet_hbm, inlet_ref, arrived.at[0, count])
    index_copy = pltpu.make_async_copy(index_hbm, index_ref, arrived.at[1, count])
    inlet_copy.start()
    for copy in cell_copies:
        copy.start()
    index_copy.start()
    for copy in state_copies:
        copy.start()
    inlet_copy.wait()
    for slot, packed_ref in enumerate(packed_refs):
        cell_copies[slot].wait()
        cells = frames_ref[slot].reshape(-1, frames_ref.shape[-1])
        drive = jnp.dot(cells, inlet_ref[...], preferred_element_type=jnp.float32)
        drive_rows = drive.shape[0]
        packed_ref[:drive_rows, :] = drive.astype(jnp.bfloat16)
        if slot == 0:
            index_copy.wait()
            index = index_ref[...].astype(jnp.bfloat16)
            blank = jnp.zeros((index.shape[0], units), jnp.bfloat16)
        state_copies[slot].wait()
        state = start_ref[slot].reshape(-1, units)
        after = drive_rows + state.shape[0]
        packed_ref[drive_rows:after, :] = state.astype(jnp.bfloat16)
        packed_ref[after:, :] = blank
        packed_ref[after:, :entries] = index


def pack_for_peers(frames, start_state, tile_index, inlet_coupler, peers, order):
    units = inlet_coupler.shape[1]
    blocks = tile_index.shape[0] * tile_index.shape[1]
    drive_rows = frames.size // frames.shape[-1] // peers
    state_rows = start_state.size // units // peers
    index = tile_index.reshape(blocks, -1)
    out_shape = (drive_rows + state_rows + blocks, units)
    share = frames.shape[1] // peers
    count = len(order)
    operands = [
        pltpu.with_memory_space_constraint(v, pltpu.HBM)
        for v in (frames, start_state, index, inlet_coupler)
    ]

    def kernel(*refs):
        inlet_kernel(order, *refs)

    return pl.pallas_call(
        kernel,
        in_specs=[pl.BlockSpec(memory_space=pltpu.HBM)] * len(operands),
        out_specs=[pl.BlockSpec(memory_space=pltpu.VMEM)] * count,
        out_shape=[pltpu.VMEM(out_shape, jnp.bfloat16)] * count,
        scratch_shapes=[
            pltpu.VMEM((count, share) + frames.shape[2:], frames.dtype),
            pltpu.VMEM((count, share) + start_state.shape[1:], start_state.dtype),
            pltpu.VMEM(index.shape, index.dtype),
            pltpu.VMEM(inlet_coupler.shape, inlet_coupler.dtype),
            pltpu.SemaphoreType.DMA((2, count + 1)),
        ],
        compiler_params=pltpu.CompilerParams(vmem_limit_bytes=VMEM_LIMIT),
    )(*operands)


def exchange(frames, start_state, tile_index, inlet_coupler, peers):
    order = partners(peers)
    got = []
    for part in (order[:1], order[1:-1], order[-1:]):
        packed = list(pack_for_peers(frames, start_state, tile_index, inlet_coupler, peers, part))
        tile_index, packed[0] = lax.optimization_barrier((tile_index, packed[0]))
        for k, block in zip(part, packed):
            if k:
                block = lax.ppermute(block, PLANE, [(p, p ^ k) for p in range(peers)])
            got.append(block)
    return got


def neighbour_choices(packed_ref, base, count_x, count_y, first_other):
    units = packed_ref.shape[-1]

    def entry(j, k):
        parts = []
        for i in range(count_x):
            rows = packed_ref[i * count_y + j, base:, :].astype(jnp.float32)
            parts.append(jnp.broadcast_to(rows[:, k : k + 1], (rows.shape[0], units)))
        return jnp.concatenate(parts, axis=0)

    columns = range(count_y)
    own = [entry(j, 0) for j in columns]
    torus_rows = own[0].shape[0]
    low = lax.broadcasted_iota(jnp.int32, own[0].shape, 0) % 2 == 0
    left = [entry(j, 3) for j in columns]
    right = [entry(j, 4) for j in columns]
    other = []
    for j in columns:
        other.append(
            [
                pltpu.roll(entry(j, 1), torus_rows - 2, axis=0),
                pltpu.roll(entry(j, 2), 2, axis=0),
                jnp.where(
                    low,
                    pltpu.roll(left[j], torus_rows - 1, axis=0),
                    pltpu.roll(left[(j + 1) % count_y], 1, axis=0),
                ),
                jnp.where(
                    low,
                    pltpu.roll(right[j - 1], torus_rows - 1, axis=0),
                    pltpu.roll(right[j], 1, axis=0),
                ),
            ]
        )

    def bits(choice):
        choice = choice.astype(jnp.int32)
        return [(choice >> bit) & 1 == 1 for bit in range(first_other.bit_length() - 1)]

    return [bits(v) for v in own], [[bits(v - first_other) for v in c] for c in other], low


def steps_kernel(count_x, count_y, torus_rows, *refs):
    got_refs, (bank_ref, sent_ref, packed_ref) = refs[:-3], refs[-3:]
    peers, rows, units = packed_ref.shape
    place = place_in_plane()
    for k, got_ref in zip(partners(peers), got_refs):
        packed_ref[place ^ k] = got_ref[...]
    home_rows = torus_rows // count_x
    trajectories = sent_ref.shape[1] // home_rows
    drive_rows = trajectories * torus_rows
    state_rows = trajectories * home_rows
    halves = bank_ref.shape[0] // 2
    groups = [(j, t) for j in range(count_y) for t in range(trajectories)]

    def choose(index, products):
        level = list(products)
        for index_bit in index:
            level = [
                jnp.where(index_bit, odd, even) for even, odd in zip(level[::2], level[1::2])
            ]
        return level[0]

    own_index, other_index, low = neighbour_choices(
        packed_ref, drive_rows + state_rows, count_x, count_y, halves
    )
    state = {}
    for j, t in groups:
        pieces = []
        for i in range(count_x):
            piece = packed_ref[i * count_y + j, drive_rows : drive_rows + state_rows, :]
            pieces.append(piece.astype(jnp.float32)[t * home_rows : (t + 1) * home_rows])
        state[j, t] = jnp.concatenate(pieces, axis=0)
    parts = min(2, trajectories)
    for step in range(count_x):
        for part in range(parts):
            members = [(j, t) for j, t in groups if t % parts == part]
            state_half = jnp.concatenate([state[g].astype(jnp.bfloat16) for g in members], axis=0)
            products = [
                jnp.dot(state_half, bank_ref[tile], preferred_element_type=jnp.float32)
                for tile in range(2 * halves)
            ]
            kept, left, right = {}, {}, {}
            for g, (j, t) in enumerate(members):
                span = slice(g * torus_rows, (g + 1) * torus_rows)
                others = [product[span] for product in products[halves:]]
                total = choose(own_index[j], [product[span] for product in products[:halves]])
                total += pltpu.roll(choose(other_index[j][0], others), 2, axis=0)
                total += pltpu.roll(choose(other_index[j][1], others), torus_rows - 2, axis=0)
                kept[j, t] = total
                left[j, t] = choose(other_index[j][2], others)
                right[j, t] = choose(other_index[j][3], others)
            for j, t in members:
                before, behind = (j - 1) % count_y, (j + 1) % count_y
                crossing = jnp.where(
                    low, left[j, t] + right[behind, t], left[before, t] + right[j, t]
                )
                total = kept[j, t] + jnp.where(
                    low,
                    pltpu.roll(crossing, torus_rows - 1, axis=0),
                    pltpu.roll(crossing, 1, axis=0),
                )
                drive = packed_ref[
                    step * count_y + j, t * torus_rows : (t + 1) * torus_rows, :
                ].astype(jnp.float32)
                state[j, t] = jnp.tanh(total + drive)
    for i in range(count_x):
        for j in range(count_y):
            pieces = []
            for t in range(trajectories):
                pieces.append(state[j, t][i * home_rows : (i + 1) * home_rows])
            sent_ref[i * count_y + j] = jnp.concatenate(pieces, axis=0).astype(jnp.bfloat16)


def run_steps(packed, tile_bank, count_x, count_y, torus_rows, home_rows):
    peers = len(packed)
    rows, units = packed[0].shape

    def kernel(*refs):
        steps_kernel(count_x, count_y, torus_rows, *refs)

    return pl.pallas_call(
        kernel,
        out_shape=jax.ShapeDtypeStruct((peers, home_rows, units), jnp.bfloat16),
        scratch_shapes=[pltpu.VMEM((peers, rows, units), jnp.bfloat16)],
        compiler_params=pltpu.CompilerParams(vmem_limit_bytes=VMEM_LIMIT),
    )(*packed, tile_bank)


def readout_kernel(state_ref, readout_ref, field_ref, final_ref):
    units = state_ref.shape[-1]
    half = state_ref[...].reshape(-1, units)
    final = half.astype(jnp.float32)
    squares = (final * final).astype(jnp.bfloat16)
    field = jnp.dot(half, readout_ref[:units], preferred_element_type=jnp.float32)
    field += jnp.dot(squares, readout_ref[units:], preferred_element_type=jnp.float32)
    final_ref[...] = final.reshape(final_ref.shape)
    field_ref[...] = field.astype(jnp.bfloat16).reshape(field_ref.shape)


def read_out(state, readout_operator, block_shape):
    return pl.pallas_call(
        readout_kernel,
        out_shape=(
            jax.ShapeDtypeStruct(block_shape + readout_operator.shape[1:], jnp.bfloat16),
            jax.ShapeDtypeStruct(block_shape + state.shape[-1:], jnp.float32),
        ),
        compiler_params=pltpu.CompilerParams(vmem_limit_bytes=VMEM_LIMIT),
    )(state, readout_operator)


def by_trajectory(frames, start_state, tile_index, tile_bank, inlet_coupler, readout_operator):
    count_x, count_y = lax.axis_size("gx"), lax.axis_size("gy")
    peers = count_x * count_y
    units = inlet_coupler.shape[1]
    block_shape = start_state.shape[:-1]
    packed = exchange(frames, start_state, tile_index, inlet_coupler, peers)
    torus_rows = frames.shape[2] * frames.shape[3]
    home_rows = start_state.size // units // peers
    sent = run_steps(packed, tile_bank, count_x, count_y, torus_rows, home_rows)
    state = lax.all_to_all(sent, PLANE, 0, 0, tiled=True)
    return read_out(state, readout_operator, block_shape)


def with_halo(cells, sides, width):
    for axis, dim in sides:
        count = lax.axis_size(axis)
        head = lax.slice_in_dim(cells, 0, width, axis=dim)
        tail = lax.slice_in_dim(cells, cells.shape[dim] - width, cells.shape[dim], axis=dim)
        cells = jnp.concatenate(
            [
                lax.ppermute(tail, axis, [(i, (i + 1) % count) for i in range(count)]),
                cells,
                lax.ppermute(head, axis, [((i + 1) % count, i) for i in range(count)]),
            ],
            axis=dim,
        )
    return cells


def by_block(frames, start_state, tile_index, tile_bank, inlet_coupler, readout_operator):
    patch_site_total = inlet_coupler.shape[0]
    hidden_node_total = inlet_coupler.shape[1]
    prediction_span = frames.shape[:-1]
    unrolled = jnp.dot(
        frames.reshape(-1, patch_site_total), inlet_coupler, preferred_element_type=jnp.float32
    )
    projected = unrolled.astype(jnp.bfloat16).reshape(prediction_span + (hidden_node_total,))
    input_signal = lax.all_to_all(projected, "gx", split_axis=2, concat_axis=0, tiled=True)
    chosen_tiles = tile_bank[tile_index]

    def advance(step_index, echo_system):
        state_half = echo_system.astype(jnp.bfloat16)
        extended = with_halo(state_half, (("gx", 1), ("gy", 2)), 1)
        adjacent_blocks = jnp.stack(
            [
                extended[:, 1:-1, 1:-1],
                extended[:, :-2, 1:-1],
                extended[:, 2:, 1:-1],
                extended[:, 1:-1, :-2],
                extended[:, 1:-1, 2:],
            ],
            axis=0,
        )
        coupled = jnp.einsum(
            "kcxyu,xykuv->cxyv", adjacent_blocks, chosen_tiles, preferred_element_type=jnp.float32
        )
        drive_now = lax.dynamic_index_in_dim(input_signal, step_index, 0, keepdims=False)
        return jnp.tanh(coupled + drive_now.astype(jnp.float32))

    echo_system = lax.fori_loop(0, input_signal.shape[0], advance, start_state)
    readout_basis = jnp.concatenate([echo_system, echo_system * echo_system], axis=-1).astype(
        jnp.bfloat16
    )
    prediction_span = readout_basis.shape[:-1]
    predicted_field = jnp.dot(
        readout_basis.reshape(-1, 2 * hidden_node_total),
        readout_operator,
        preferred_element_type=jnp.float32,
    )
    predicted_field = predicted_field.astype(jnp.bfloat16).reshape(
        prediction_span + (patch_site_total,)
    )
    return (predicted_field, echo_system)


def solution(mesh):
    placed = (
        P("gx", ("groups", "ta"), None, "gy", None),
        P(("groups", "ta"), "gx", "gy", None),
        P("gx", "gy", None),
        P(),
        P(),
        P(),
    )
    def shards(frames, start_state, *rest):
        peers = mesh.shape["gx"] * mesh.shape["gy"]
        fits = start_state.shape[0] % peers == 0 and peers & (peers - 1) == 0 and start_state.shape[2] == 2
        fits = fits and start_state.shape[1] % 4 == 0
        body = by_trajectory if fits and frames.shape[0] == 1 else by_block
        return body(frames, start_state, *rest)

    return jax.shard_map(
        shards,
        mesh=mesh,
        in_specs=placed,
        out_specs=(P(("groups", "ta"), "gx", "gy", None), P(("groups", "ta"), "gx", "gy", None)),
        check_vma=False,
    )
```

```python
import jax
import jax.numpy as jnp
from jax import lax
from jax.experimental import pallas as pl
from jax.experimental.pallas import tpu as pltpu
from jax.sharding import PartitionSpec as P

PLANE = ("gx", "gy")
LANES = 128
VMEM_LIMIT = 24 * 1024 * 1024


def whole(shape):
    return pl.BlockSpec(shape, lambda *_: (0,) * len(shape))


def place_in_plane():
    return lax.axis_index("gx") * lax.axis_size("gy") + lax.axis_index("gy")


def place_in_plane():
    return lax.axis_index("gx") * lax.axis_size("gy") + lax.axis_index("gy")


def partners(peers):
    return sorted(range(peers), key=lambda k: (-k.bit_count(), -k))


def return_flip(peers):
    return peers // 2 + 1 if peers > 2 else 0


def store_rows(ref, at, rows):
    for piece in range(rows.shape[1] // LANES):
        ref[at : at + rows.shape[0], :] = rows[:, piece * LANES : (piece + 1) * LANES]
        at += rows.shape[0]
    return at


def load_rows(ref, block, at, first, count, rows, units):
    pieces = []
    for piece in range(units // LANES):
        start = at + piece * rows + first
        pieces.append(ref[block, start : start + count, :])
    return jnp.concatenate(pieces, axis=1)


def inlet_kernel(order, frames_hbm, start_hbm, index_hbm, inlet_hbm, *refs):
    count = len(order)
    packed_refs, (frames_ref, start_ref, index_ref, inlet_ref, arrived) = refs[:count], refs[count:]
    units = inlet_ref.shape[1]
    place = place_in_plane()
    share = frames_ref.shape[1]
    entries = index_ref.shape[-1]
    cell_copies, state_copies = [], []
    for slot, k in enumerate(order):
        mine = pl.ds((place ^ k) * share, share)
        cell_copies.append(
            pltpu.make_async_copy(frames_hbm.at[0, mine], frames_ref.at[slot], arrived.at[0, slot])
        )
        state_copies.append(
            pltpu.make_async_copy(start_hbm.at[mine], start_ref.at[slot], arrived.at[1, slot])
        )
    inlet_copy = pltpu.make_async_copy(inlet_hbm, inlet_ref, arrived.at[0, count])
    index_copy = pltpu.make_async_copy(index_hbm, index_ref, arrived.at[1, count])
    inlet_copy.start()
    for copy in cell_copies:
        copy.start()
    index_copy.start()
    for copy in state_copies:
        copy.start()
    inlet_copy.wait()
    for slot, packed_ref in enumerate(packed_refs):
        cell_copies[slot].wait()
        cells = frames_ref[slot].reshape(-1, frames_ref.shape[-1])
        drive = jnp.dot(cells, inlet_ref[...], preferred_element_type=jnp.float32)
        after = store_rows(packed_ref, 0, drive.astype(jnp.bfloat16))
        if slot == 0:
            index_copy.wait()
            index = index_ref[...].astype(jnp.bfloat16)
            blank = jnp.zeros((index.shape[0], packed_ref.shape[1]), jnp.bfloat16)
        state_copies[slot].wait()
        state = start_ref[slot].reshape(-1, units)
        after = store_rows(packed_ref, after, state.astype(jnp.bfloat16))
        packed_ref[after:, :] = blank
        packed_ref[after:, :entries] = index


def pack_for_peers(frames, start_state, tile_index, inlet_coupler, peers, order):
    units = inlet_coupler.shape[1]
    blocks = tile_index.shape[0] * tile_index.shape[1]
    drive_rows = frames.size // frames.shape[-1] // peers
    state_rows = start_state.size // units // peers
    index = tile_index.reshape(blocks, -1)
    out_shape = ((drive_rows + state_rows) * units // LANES + blocks, LANES)
    share = frames.shape[1] // peers
    count = len(order)
    operands = [
        pltpu.with_memory_space_constraint(v, pltpu.HBM)
        for v in (frames, start_state, index, inlet_coupler)
    ]

    def kernel(*refs):
        inlet_kernel(order, *refs)

    return pl.pallas_call(
        kernel,
        in_specs=[pl.BlockSpec(memory_space=pltpu.HBM)] * len(operands),
        out_specs=[pl.BlockSpec(memory_space=pltpu.VMEM)] * count,
        out_shape=[pltpu.VMEM(out_shape, jnp.bfloat16)] * count,
        scratch_shapes=[
            pltpu.VMEM((count, share) + frames.shape[2:], frames.dtype),
            pltpu.VMEM((count, share) + start_state.shape[1:], start_state.dtype),
            pltpu.VMEM(index.shape, index.dtype),
            pltpu.VMEM(inlet_coupler.shape, inlet_coupler.dtype),
            pltpu.SemaphoreType.DMA((2, count + 1)),
        ],
        compiler_params=pltpu.CompilerParams(vmem_limit_bytes=VMEM_LIMIT),
    )(*operands)


def exchange(frames, start_state, tile_index, inlet_coupler, peers):
    order = partners(peers)
    got = []
    for part in (order[:1], order[1:-1], order[-1:]):
        packed = list(pack_for_peers(frames, start_state, tile_index, inlet_coupler, peers, part))
        tile_index, packed[0] = lax.optimization_barrier((tile_index, packed[0]))
        for k, block in zip(part, packed):
            if k:
                block = lax.ppermute(block, PLANE, [(p, p ^ k) for p in range(peers)])
            got.append(block)
    return got


def neighbour_choices(packed_ref, base, units, count_x, count_y, first_other):
    def entry(j, k):
        parts = []
        for i in range(count_x):
            rows = packed_ref[i * count_y + j, base:, :].astype(jnp.float32)
            parts.append(jnp.broadcast_to(rows[:, k : k + 1], (rows.shape[0], units)))
        return jnp.concatenate(parts, axis=0)

    columns = range(count_y)
    own = [entry(j, 0) for j in columns]
    torus_rows = own[0].shape[0]
    low = lax.broadcasted_iota(jnp.int32, own[0].shape, 0) % 2 == 0
    left = [entry(j, 3) for j in columns]
    right = [entry(j, 4) for j in columns]
    other = []
    for j in columns:
        other.append(
            [
                pltpu.roll(entry(j, 1), torus_rows - 2, axis=0),
                pltpu.roll(entry(j, 2), 2, axis=0),
                jnp.where(
                    low,
                    pltpu.roll(left[j], torus_rows - 1, axis=0),
                    pltpu.roll(left[(j + 1) % count_y], 1, axis=0),
                ),
                jnp.where(
                    low,
                    pltpu.roll(right[j - 1], torus_rows - 1, axis=0),
                    pltpu.roll(right[j], 1, axis=0),
                ),
            ]
        )

    def bits(choice):
        choice = choice.astype(jnp.int32)
        return [(choice >> bit) & 1 == 1 for bit in range(first_other.bit_length() - 1)]

    return [bits(v) for v in own], [[bits(v - first_other) for v in c] for c in other], low


def steps_kernel(count_x, count_y, torus_rows, *refs):
    got_refs, (bank_ref, sent_ref, packed_ref) = refs[:-3], refs[-3:]
    peers, units = packed_ref.shape[0], bank_ref.shape[-1]
    place = place_in_plane()
    for k, got_ref in zip(partners(peers), got_refs):
        packed_ref[place ^ k] = got_ref[...]
    home_rows = torus_rows // count_x
    trajectories = sent_ref.shape[1] // home_rows
    drive_rows = trajectories * torus_rows
    state_rows = trajectories * home_rows
    halves = bank_ref.shape[0] // 2
    groups = [(j, t) for j in range(count_y) for t in range(trajectories)]

    def choose(index, products):
        level = list(products)
        for index_bit in index:
            level = [
                jnp.where(index_bit, odd, even) for even, odd in zip(level[::2], level[1::2])
            ]
        return level[0]

    own_index, other_index, low = neighbour_choices(
        packed_ref, (drive_rows + state_rows) * units // LANES, units, count_x, count_y, halves
    )
    state = {}
    for j, t in groups:
        pieces = []
        for i in range(count_x):
            piece = load_rows(
                packed_ref, i * count_y + j, drive_rows * units // LANES, 0, state_rows, state_rows, units
            )
            pieces.append(piece.astype(jnp.float32)[t * home_rows : (t + 1) * home_rows])
        state[j, t] = jnp.concatenate(pieces, axis=0)
    parts = min(2, trajectories)
    for step in range(count_x):
        for part in range(parts):
            members = [(j, t) for j, t in groups if t % parts == part]
            state_half = jnp.concatenate([state[g].astype(jnp.bfloat16) for g in members], axis=0)
            products = [
                jnp.dot(state_half, bank_ref[tile], preferred_element_type=jnp.float32)
                for tile in range(2 * halves)
            ]
            kept, left, right = {}, {}, {}
            for g, (j, t) in enumerate(members):
                span = slice(g * torus_rows, (g + 1) * torus_rows)
                others = [product[span] for product in products[halves:]]
                total = choose(own_index[j], [product[span] for product in products[:halves]])
                total += pltpu.roll(choose(other_index[j][0], others), 2, axis=0)
                total += pltpu.roll(choose(other_index[j][1], others), torus_rows - 2, axis=0)
                kept[j, t] = total
                left[j, t] = choose(other_index[j][2], others)
                right[j, t] = choose(other_index[j][3], others)
            for j, t in members:
                before, behind = (j - 1) % count_y, (j + 1) % count_y
                crossing = jnp.where(
                    low, left[j, t] + right[behind, t], left[before, t] + right[j, t]
                )
                total = kept[j, t] + jnp.where(
                    low,
                    pltpu.roll(crossing, torus_rows - 1, axis=0),
                    pltpu.roll(crossing, 1, axis=0),
                )
                drive = load_rows(
                    packed_ref, step * count_y + j, 0, t * torus_rows, torus_rows, drive_rows, units
                )
                state[j, t] = jnp.tanh(total + drive.astype(jnp.float32))
    for i in range(count_x):
        for j in range(count_y):
            pieces = []
            for t in range(trajectories):
                pieces.append(state[j, t][i * home_rows : (i + 1) * home_rows])
            sent_ref[(i * count_y + j) ^ return_flip(peers)] = jnp.concatenate(pieces, axis=0).astype(jnp.bfloat16)


def run_steps(packed, tile_bank, count_x, count_y, torus_rows, home_rows):
    peers, units = len(packed), tile_bank.shape[-1]

    def kernel(*refs):
        steps_kernel(count_x, count_y, torus_rows, *refs)

    return pl.pallas_call(
        kernel,
        out_shape=jax.ShapeDtypeStruct((peers, home_rows, units), jnp.bfloat16),
        scratch_shapes=[pltpu.VMEM((peers,) + packed[0].shape, jnp.bfloat16)],
        compiler_params=pltpu.CompilerParams(vmem_limit_bytes=VMEM_LIMIT),
    )(*packed, tile_bank)


def readout_kernel(state_ref, readout_ref, field_ref, final_ref):
    units = state_ref.shape[-1]
    peers = state_ref.shape[0]
    half = jnp.concatenate([state_ref[p ^ return_flip(peers)] for p in range(peers)], axis=0)
    final = half.astype(jnp.float32)
    squares = (final * final).astype(jnp.bfloat16)
    field = jnp.dot(half, readout_ref[:units], preferred_element_type=jnp.float32)
    field += jnp.dot(squares, readout_ref[units:], preferred_element_type=jnp.float32)
    final_ref[...] = final.reshape(final_ref.shape)
    field_ref[...] = field.astype(jnp.bfloat16).reshape(field_ref.shape)


def read_out(state, readout_operator, block_shape):
    return pl.pallas_call(
        readout_kernel,
        out_shape=(
            jax.ShapeDtypeStruct(block_shape + readout_operator.shape[1:], jnp.bfloat16),
            jax.ShapeDtypeStruct(block_shape + state.shape[-1:], jnp.float32),
        ),
        compiler_params=pltpu.CompilerParams(vmem_limit_bytes=VMEM_LIMIT),
    )(state, readout_operator)


def by_trajectory(frames, start_state, tile_index, tile_bank, inlet_coupler, readout_operator):
    count_x, count_y = lax.axis_size("gx"), lax.axis_size("gy")
    peers = count_x * count_y
    units = inlet_coupler.shape[1]
    block_shape = start_state.shape[:-1]
    packed = exchange(frames, start_state, tile_index, inlet_coupler, peers)
    torus_rows = frames.shape[2] * frames.shape[3]
    home_rows = start_state.size // units // peers
    sent = run_steps(packed, tile_bank, count_x, count_y, torus_rows, home_rows)
    group = [p ^ return_flip(peers) for p in range(peers)]
    state = lax.all_to_all(sent, PLANE, 0, 0, tiled=True, axis_index_groups=[group])
    return read_out(state, readout_operator, block_shape)


def with_halo(cells, sides, width):
    for axis, dim in sides:
        count = lax.axis_size(axis)
        head = lax.slice_in_dim(cells, 0, width, axis=dim)
        tail = lax.slice_in_dim(cells, cells.shape[dim] - width, cells.shape[dim], axis=dim)
        cells = jnp.concatenate(
            [
                lax.ppermute(tail, axis, [(i, (i + 1) % count) for i in range(count)]),
                cells,
                lax.ppermute(head, axis, [((i + 1) % count, i) for i in range(count)]),
            ],
            axis=dim,
        )
    return cells


def by_block(frames, start_state, tile_index, tile_bank, inlet_coupler, readout_operator):
    patch_site_total = inlet_coupler.shape[0]
    hidden_node_total = inlet_coupler.shape[1]
    prediction_span = frames.shape[:-1]
    unrolled = jnp.dot(
        frames.reshape(-1, patch_site_total), inlet_coupler, preferred_element_type=jnp.float32
    )
    projected = unrolled.astype(jnp.bfloat16).reshape(prediction_span + (hidden_node_total,))
    input_signal = lax.all_to_all(projected, "gx", split_axis=2, concat_axis=0, tiled=True)
    chosen_tiles = tile_bank[tile_index]

    def advance(step_index, echo_system):
        state_half = echo_system.astype(jnp.bfloat16)
        extended = with_halo(state_half, (("gx", 1), ("gy", 2)), 1)
        adjacent_blocks = jnp.stack(
            [
                extended[:, 1:-1, 1:-1],
                extended[:, :-2, 1:-1],
                extended[:, 2:, 1:-1],
                extended[:, 1:-1, :-2],
                extended[:, 1:-1, 2:],
            ],
            axis=0,
        )
        coupled = jnp.einsum(
            "kcxyu,xykuv->cxyv", adjacent_blocks, chosen_tiles, preferred_element_type=jnp.float32
        )
        drive_now = lax.dynamic_index_in_dim(input_signal, step_index, 0, keepdims=False)
        return jnp.tanh(coupled + drive_now.astype(jnp.float32))

    echo_system = lax.fori_loop(0, input_signal.shape[0], advance, start_state)
    readout_basis = jnp.concatenate([echo_system, echo_system * echo_system], axis=-1).astype(
        jnp.bfloat16
    )
    prediction_span = readout_basis.shape[:-1]
    predicted_field = jnp.dot(
        readout_basis.reshape(-1, 2 * hidden_node_total),
        readout_operator,
        preferred_element_type=jnp.float32,
    )
    predicted_field = predicted_field.astype(jnp.bfloat16).reshape(
        prediction_span + (patch_site_total,)
    )
    return (predicted_field, echo_system)


def solution(mesh):
    placed = (
        P("gx", ("groups", "ta"), None, "gy", None),
        P(("groups", "ta"), "gx", "gy", None),
        P("gx", "gy", None),
        P(),
        P(),
        P(),
    )
    def shards(frames, start_state, *rest):
        peers = mesh.shape["gx"] * mesh.shape["gy"]
        fits = start_state.shape[0] % peers == 0 and peers & (peers - 1) == 0 and start_state.shape[2] == 2
        fits = fits and start_state.shape[1] % 4 == 0
        body = by_trajectory if fits and frames.shape[0] == 1 else by_block
        return body(frames, start_state, *rest)

    return jax.shard_map(
        shards,
        mesh=mesh,
        in_specs=placed,
        out_specs=(P(("groups", "ta"), "gx", "gy", None), P(("groups", "ta"), "gx", "gy", None)),
        check_vma=False,
    )
```

```python
import jax
import jax.numpy as jnp
from jax import lax
from jax.experimental import pallas as pl
from jax.experimental.pallas import tpu as pltpu
from jax.sharding import PartitionSpec as P

PLANE = ("gx", "gy")
LANES = 128
VMEM_LIMIT = 24 * 1024 * 1024


def whole(shape):
    return pl.BlockSpec(shape, lambda *_: (0,) * len(shape))


def place_in_plane():
    return lax.axis_index("gx") * lax.axis_size("gy") + lax.axis_index("gy")


def place_in_plane():
    return lax.axis_index("gx") * lax.axis_size("gy") + lax.axis_index("gy")


def partners(peers):
    served = (6, 7, 2, 5, 3, 4, 1)
    return sorted(range(1, peers), key=lambda k: served.index(k) if k in served else k) + [0]


def return_flip(peers):
    return peers // 2 + 1 if peers > 2 else 0


def store_rows(ref, at, rows):
    for piece in range(rows.shape[1] // LANES):
        ref[at : at + rows.shape[0], :] = rows[:, piece * LANES : (piece + 1) * LANES]
        at += rows.shape[0]
    return at


def load_rows(ref, block, at, first, count, rows, units):
    pieces = []
    for piece in range(units // LANES):
        start = at + piece * rows + first
        pieces.append(ref[block, start : start + count, :])
    return jnp.concatenate(pieces, axis=1)


def inlet_kernel(order, frames_hbm, start_hbm, index_hbm, inlet_hbm, *refs):
    count = len(order)
    packed_refs, (frames_ref, start_ref, index_ref, inlet_ref, arrived) = refs[:count], refs[count:]
    units = inlet_ref.shape[1]
    place = place_in_plane()
    share = frames_ref.shape[1]
    entries = index_ref.shape[-1]
    cell_copies, state_copies = [], []
    for slot, k in enumerate(order):
        mine = pl.ds((place ^ k) * share, share)
        cell_copies.append(
            pltpu.make_async_copy(frames_hbm.at[0, mine], frames_ref.at[slot], arrived.at[0, slot])
        )
        state_copies.append(
            pltpu.make_async_copy(start_hbm.at[mine], start_ref.at[slot], arrived.at[1, slot])
        )
    inlet_copy = pltpu.make_async_copy(inlet_hbm, inlet_ref, arrived.at[0, count])
    index_copy = pltpu.make_async_copy(index_hbm, index_ref, arrived.at[1, count])
    inlet_copy.start()
    for copy in cell_copies:
        copy.start()
    index_copy.start()
    for copy in state_copies:
        copy.start()
    inlet_copy.wait()
    for slot, packed_ref in enumerate(packed_refs):
        cell_copies[slot].wait()
        cells = frames_ref[slot].reshape(-1, frames_ref.shape[-1])
        drive = jnp.dot(cells, inlet_ref[...], preferred_element_type=jnp.float32)
        after = store_rows(packed_ref, 0, drive.astype(jnp.bfloat16))
        if slot == 0:
            index_copy.wait()
            index = index_ref[...].astype(jnp.bfloat16)
            blank = jnp.zeros((index.shape[0], packed_ref.shape[1]), jnp.bfloat16)
        state_copies[slot].wait()
        state = start_ref[slot].reshape(-1, units)
        after = store_rows(packed_ref, after, state.astype(jnp.bfloat16))
        packed_ref[after:, :] = blank
        packed_ref[after:, :entries] = index


def pack_for_peers(frames, start_state, tile_index, inlet_coupler, peers, order):
    units = inlet_coupler.shape[1]
    blocks = tile_index.shape[0] * tile_index.shape[1]
    drive_rows = frames.size // frames.shape[-1] // peers
    state_rows = start_state.size // units // peers
    index = tile_index.reshape(blocks, -1)
    out_shape = ((drive_rows + state_rows) * units // LANES + blocks, LANES)
    share = frames.shape[1] // peers
    count = len(order)
    operands = [
        pltpu.with_memory_space_constraint(v, pltpu.HBM)
        for v in (frames, start_state, index, inlet_coupler)
    ]

    def kernel(*refs):
        inlet_kernel(order, *refs)

    return pl.pallas_call(
        kernel,
        in_specs=[pl.BlockSpec(memory_space=pltpu.HBM)] * len(operands),
        out_specs=[pl.BlockSpec(memory_space=pltpu.VMEM)] * count,
        out_shape=[pltpu.VMEM(out_shape, jnp.bfloat16)] * count,
        scratch_shapes=[
            pltpu.VMEM((count, share) + frames.shape[2:], frames.dtype),
            pltpu.VMEM((count, share) + start_state.shape[1:], start_state.dtype),
            pltpu.VMEM(index.shape, index.dtype),
            pltpu.VMEM(inlet_coupler.shape, inlet_coupler.dtype),
            pltpu.SemaphoreType.DMA((2, count + 1)),
        ],
        compiler_params=pltpu.CompilerParams(vmem_limit_bytes=VMEM_LIMIT),
    )(*operands)


def exchange(frames, start_state, tile_index, inlet_coupler, peers):
    order = partners(peers)
    got = []
    for part in (order[:1], order[1:-1], order[-1:]):
        packed = list(pack_for_peers(frames, start_state, tile_index, inlet_coupler, peers, part))
        tile_index, packed[0] = lax.optimization_barrier((tile_index, packed[0]))
        for k, block in zip(part, packed):
            if k:
                block = lax.ppermute(block, PLANE, [(p, p ^ k) for p in range(peers)])
            got.append(block)
    return got


def neighbour_choices(packed_ref, base, count_x, count_y, first_other):
    def entry(j, k):
        parts = []
        for i in range(count_x):
            rows = packed_ref[i * count_y + j, base:, :].astype(jnp.float32)
            parts.append(jnp.broadcast_to(rows[:, k : k + 1], (rows.shape[0], LANES)))
        return jnp.concatenate(parts, axis=0)

    columns = range(count_y)
    own = [entry(j, 0) for j in columns]
    torus_rows = own[0].shape[0]
    low = lax.broadcasted_iota(jnp.int32, own[0].shape, 0) % 2 == 0
    left = [entry(j, 3) for j in columns]
    right = [entry(j, 4) for j in columns]
    other = []
    for j in columns:
        other.append(
            [
                pltpu.roll(entry(j, 1), torus_rows - 2, axis=0),
                pltpu.roll(entry(j, 2), 2, axis=0),
                jnp.where(
                    low,
                    pltpu.roll(left[j], torus_rows - 1, axis=0),
                    pltpu.roll(left[(j + 1) % count_y], 1, axis=0),
                ),
                jnp.where(
                    low,
                    pltpu.roll(right[j - 1], torus_rows - 1, axis=0),
                    pltpu.roll(right[j], 1, axis=0),
                ),
            ]
        )

    def bits(choice):
        choice = choice.astype(jnp.int32)
        return [(choice >> bit) & 1 == 1 for bit in range(first_other.bit_length() - 1)]

    shares = [[(v == tile).astype(jnp.bfloat16) for tile in range(first_other)] for v in own]
    return shares, [[bits(v - first_other) for v in c] for c in other]


def steps_kernel(count_x, count_y, torus_rows, *refs):
    got_refs, (bank_ref, sent_ref, packed_ref) = refs[:-3], refs[-3:]
    peers, units = packed_ref.shape[0], bank_ref.shape[-1]
    place = place_in_plane()
    for k, got_ref in zip(partners(peers), got_refs):
        packed_ref[place ^ k] = got_ref[...]
    home_rows = torus_rows // count_x
    trajectories = sent_ref.shape[1] // home_rows
    drive_rows = trajectories * torus_rows
    state_rows = trajectories * home_rows
    halves = bank_ref.shape[0] // 2
    groups = [(j, t) for j in range(count_y) for t in range(trajectories)]

    def choose(index, products):
        chosen = []
        for piece in range(units // LANES):
            level = [product[:, piece * LANES : (piece + 1) * LANES] for product in products]
            for index_bit in index:
                level = [
                    jnp.where(index_bit, odd, even) for even, odd in zip(level[::2], level[1::2])
                ]
            chosen.append(level[0])
        return jnp.concatenate(chosen, axis=1)

    low = lax.broadcasted_iota(jnp.int32, (torus_rows, units), 0) % 2 == 0

    def share_of(rows, share):
        return rows.astype(jnp.bfloat16) * jnp.concatenate([share] * (units // LANES), axis=1)

    own_share, other_index = neighbour_choices(
        packed_ref, (drive_rows + state_rows) * units // LANES, count_x, count_y, halves
    )
    state = {}
    for j, t in groups:
        pieces = []
        for i in range(count_x):
            piece = load_rows(
                packed_ref, i * count_y + j, drive_rows * units // LANES, 0, state_rows, state_rows, units
            )
            pieces.append(piece.astype(jnp.float32)[t * home_rows : (t + 1) * home_rows])
        state[j, t] = jnp.concatenate(pieces, axis=0)
    parts = min(2, trajectories)
    for step in range(count_x):
        for part in range(parts):
            members = [(j, t) for j, t in groups if t % parts == part]
            state_half = jnp.concatenate([state[g].astype(jnp.bfloat16) for g in members], axis=0)
            masked = [
                jnp.concatenate([share_of(state[j, t], own_share[j][tile]) for j, t in members], axis=0)
                for tile in range(halves)
            ]
            own = jnp.dot(
                jnp.concatenate(masked, axis=1),
                bank_ref[:halves].reshape(halves * units, units),
                preferred_element_type=jnp.float32,
            )
            products = [
                jnp.dot(state_half, bank_ref[halves + tile], preferred_element_type=jnp.float32)
                for tile in range(halves)
            ]
            kept, left, right = {}, {}, {}
            for g, (j, t) in enumerate(members):
                span = slice(g * torus_rows, (g + 1) * torus_rows)
                others = [product[span] for product in products]
                total = own[span]
                total += pltpu.roll(choose(other_index[j][0], others), 2, axis=0)
                total += pltpu.roll(choose(other_index[j][1], others), torus_rows - 2, axis=0)
                kept[j, t] = total
                left[j, t] = choose(other_index[j][2], others)
                right[j, t] = choose(other_index[j][3], others)
            for j, t in members:
                before, behind = (j - 1) % count_y, (j + 1) % count_y
                crossing = jnp.where(
                    low, left[j, t] + right[behind, t], left[before, t] + right[j, t]
                )
                total = kept[j, t] + jnp.where(
                    low,
                    pltpu.roll(crossing, torus_rows - 1, axis=0),
                    pltpu.roll(crossing, 1, axis=0),
                )
                drive = load_rows(
                    packed_ref, step * count_y + j, 0, t * torus_rows, torus_rows, drive_rows, units
                )
                state[j, t] = jnp.tanh(total + drive.astype(jnp.float32))
    for i in range(count_x):
        for j in range(count_y):
            pieces = []
            for t in range(trajectories):
                pieces.append(state[j, t][i * home_rows : (i + 1) * home_rows])
            sent_ref[(i * count_y + j) ^ return_flip(peers)] = jnp.concatenate(pieces, axis=0).astype(jnp.bfloat16)


def run_steps(packed, tile_bank, count_x, count_y, torus_rows, home_rows):
    peers, units = len(packed), tile_bank.shape[-1]

    def kernel(*refs):
        steps_kernel(count_x, count_y, torus_rows, *refs)

    return pl.pallas_call(
        kernel,
        out_shape=jax.ShapeDtypeStruct((peers, home_rows, units), jnp.bfloat16),
        scratch_shapes=[pltpu.VMEM((peers,) + packed[0].shape, jnp.bfloat16)],
        compiler_params=pltpu.CompilerParams(vmem_limit_bytes=VMEM_LIMIT),
    )(*packed, tile_bank)


def readout_kernel(state_ref, readout_ref, field_ref, final_ref):
    units = state_ref.shape[-1]
    peers = state_ref.shape[0]
    half = jnp.concatenate([state_ref[p ^ return_flip(peers)] for p in range(peers)], axis=0)
    final = half.astype(jnp.float32)
    squares = (final * final).astype(jnp.bfloat16)
    field = jnp.dot(half, readout_ref[:units], preferred_element_type=jnp.float32)
    field += jnp.dot(squares, readout_ref[units:], preferred_element_type=jnp.float32)
    final_ref[...] = final.reshape(final_ref.shape)
    field_ref[...] = field.astype(jnp.bfloat16).reshape(field_ref.shape)


def read_out(state, readout_operator, block_shape):
    return pl.pallas_call(
        readout_kernel,
        out_shape=(
            jax.ShapeDtypeStruct(block_shape + readout_operator.shape[1:], jnp.bfloat16),
            jax.ShapeDtypeStruct(block_shape + state.shape[-1:], jnp.float32),
        ),
        compiler_params=pltpu.CompilerParams(vmem_limit_bytes=VMEM_LIMIT),
    )(state, readout_operator)


def by_trajectory(frames, start_state, tile_index, tile_bank, inlet_coupler, readout_operator):
    count_x, count_y = lax.axis_size("gx"), lax.axis_size("gy")
    peers = count_x * count_y
    units = inlet_coupler.shape[1]
    block_shape = start_state.shape[:-1]
    packed = exchange(frames, start_state, tile_index, inlet_coupler, peers)
    torus_rows = frames.shape[2] * frames.shape[3]
    home_rows = start_state.size // units // peers
    sent = run_steps(packed, tile_bank, count_x, count_y, torus_rows, home_rows)
    group = [p ^ return_flip(peers) for p in range(peers)]
    state = lax.all_to_all(sent, PLANE, 0, 0, tiled=True, axis_index_groups=[group])
    return read_out(state, readout_operator, block_shape)


def with_halo(cells, sides, width):
    for axis, dim in sides:
        count = lax.axis_size(axis)
        head = lax.slice_in_dim(cells, 0, width, axis=dim)
        tail = lax.slice_in_dim(cells, cells.shape[dim] - width, cells.shape[dim], axis=dim)
        cells = jnp.concatenate(
            [
                lax.ppermute(tail, axis, [(i, (i + 1) % count) for i in range(count)]),
                cells,
                lax.ppermute(head, axis, [((i + 1) % count, i) for i in range(count)]),
            ],
            axis=dim,
        )
    return cells


def by_block(frames, start_state, tile_index, tile_bank, inlet_coupler, readout_operator):
    patch_site_total = inlet_coupler.shape[0]
    hidden_node_total = inlet_coupler.shape[1]
    prediction_span = frames.shape[:-1]
    unrolled = jnp.dot(
        frames.reshape(-1, patch_site_total), inlet_coupler, preferred_element_type=jnp.float32
    )
    projected = unrolled.astype(jnp.bfloat16).reshape(prediction_span + (hidden_node_total,))
    input_signal = lax.all_to_all(projected, "gx", split_axis=2, concat_axis=0, tiled=True)
    chosen_tiles = tile_bank[tile_index]

    def advance(step_index, echo_system):
        state_half = echo_system.astype(jnp.bfloat16)
        extended = with_halo(state_half, (("gx", 1), ("gy", 2)), 1)
        adjacent_blocks = jnp.stack(
            [
                extended[:, 1:-1, 1:-1],
                extended[:, :-2, 1:-1],
                extended[:, 2:, 1:-1],
                extended[:, 1:-1, :-2],
                extended[:, 1:-1, 2:],
            ],
            axis=0,
        )
        coupled = jnp.einsum(
            "kcxyu,xykuv->cxyv", adjacent_blocks, chosen_tiles, preferred_element_type=jnp.float32
        )
        drive_now = lax.dynamic_index_in_dim(input_signal, step_index, 0, keepdims=False)
        return jnp.tanh(coupled + drive_now.astype(jnp.float32))

    echo_system = lax.fori_loop(0, input_signal.shape[0], advance, start_state)
    readout_basis = jnp.concatenate([echo_system, echo_system * echo_system], axis=-1).astype(
        jnp.bfloat16
    )
    prediction_span = readout_basis.shape[:-1]
    predicted_field = jnp.dot(
        readout_basis.reshape(-1, 2 * hidden_node_total),
        readout_operator,
        preferred_element_type=jnp.float32,
    )
    predicted_field = predicted_field.astype(jnp.bfloat16).reshape(
        prediction_span + (patch_site_total,)
    )
    return (predicted_field, echo_system)


def solution(mesh):
    placed = (
        P("gx", ("groups", "ta"), None, "gy", None),
        P(("groups", "ta"), "gx", "gy", None),
        P("gx", "gy", None),
        P(),
        P(),
        P(),
    )
    def shards(frames, start_state, tile_index, tile_bank, *rest):
        peers = mesh.shape["gx"] * mesh.shape["gy"]
        halves = tile_bank.shape[0] // 2
        fits = all(v & (v - 1) == 0 for v in (peers, halves))
        fits = fits and start_state.shape[0] % peers == 0 and start_state.shape[1] % 4 == 0
        fits = fits and start_state.shape[2] == 2 and start_state.shape[3] % LANES == 0
        body = by_trajectory if fits and frames.shape[0] == 1 else by_block
        return body(frames, start_state, tile_index, tile_bank, *rest)

    return jax.shard_map(
        shards,
        mesh=mesh,
        in_specs=placed,
        out_specs=(P(("groups", "ta"), "gx", "gy", None), P(("groups", "ta"), "gx", "gy", None)),
        check_vma=False,
    )
```

```python
import jax
import jax.numpy as jnp
from jax import lax
from jax.experimental import pallas as pl
from jax.experimental.pallas import tpu as pltpu
from jax.sharding import PartitionSpec as P

PLANE = ("gx", "gy")
LANES = 128
VMEM_LIMIT = 24 * 1024 * 1024


def whole(shape):
    return pl.BlockSpec(shape, lambda *_: (0,) * len(shape))


def place_in_plane():
    return lax.axis_index("gx") * lax.axis_size("gy") + lax.axis_index("gy")


def place_in_plane():
    return lax.axis_index("gx") * lax.axis_size("gy") + lax.axis_index("gy")


def partners(peers):
    served = (6, 7, 2, 5, 3, 4, 1)
    return sorted(range(1, peers), key=lambda k: served.index(k) if k in served else k) + [0]


def return_flip(peers):
    return peers // 2 + 1 if peers > 2 else 0


def store_rows(ref, at, rows):
    for piece in range(rows.shape[1] // LANES):
        ref[at : at + rows.shape[0], :] = rows[:, piece * LANES : (piece + 1) * LANES]
        at += rows.shape[0]
    return at


def load_rows(ref, block, at, first, count, rows, units):
    pieces = []
    for piece in range(units // LANES):
        start = at + piece * rows + first
        pieces.append(ref[block, start : start + count, :])
    return jnp.concatenate(pieces, axis=1)


def inlet_kernel(order, frames_hbm, start_hbm, index_hbm, inlet_hbm, *refs):
    count = len(order)
    packed_refs, (frames_ref, start_ref, index_ref, inlet_ref, arrived) = refs[:count], refs[count:]
    units = inlet_ref.shape[1]
    place = place_in_plane()
    share = frames_ref.shape[1]
    entries = index_ref.shape[-1]
    cell_copies, state_copies = [], []
    for slot, k in enumerate(order):
        mine = pl.ds((place ^ k) * share, share)
        cell_copies.append(
            pltpu.make_async_copy(frames_hbm.at[0, mine], frames_ref.at[slot], arrived.at[0, slot])
        )
        state_copies.append(
            pltpu.make_async_copy(start_hbm.at[mine], start_ref.at[slot], arrived.at[1, slot])
        )
    inlet_copy = pltpu.make_async_copy(inlet_hbm, inlet_ref, arrived.at[0, count])
    index_copy = pltpu.make_async_copy(index_hbm, index_ref, arrived.at[1, count])
    inlet_copy.start()
    for copy in cell_copies:
        copy.start()
    index_copy.start()
    for copy in state_copies:
        copy.start()
    inlet_copy.wait()
    for slot, packed_ref in enumerate(packed_refs):
        cell_copies[slot].wait()
        cells = frames_ref[slot].reshape(-1, frames_ref.shape[-1])
        drive = jnp.dot(cells, inlet_ref[...], preferred_element_type=jnp.float32)
        after = store_rows(packed_ref, 0, drive.astype(jnp.bfloat16))
        if slot == 0:
            index_copy.wait()
            index = index_ref[...].astype(jnp.bfloat16)
            blank = jnp.zeros((index.shape[0], packed_ref.shape[1]), jnp.bfloat16)
        state_copies[slot].wait()
        state = start_ref[slot].reshape(-1, units)
        after = store_rows(packed_ref, after, state.astype(jnp.bfloat16))
        packed_ref[after:, :] = blank
        packed_ref[after:, :entries] = index


def pack_for_peers(frames, start_state, tile_index, inlet_coupler, peers, order):
    units = inlet_coupler.shape[1]
    blocks = tile_index.shape[0] * tile_index.shape[1]
    drive_rows = frames.size // frames.shape[-1] // peers
    state_rows = start_state.size // units // peers
    index = tile_index.reshape(blocks, -1)
    out_shape = ((drive_rows + state_rows) * units // LANES + blocks, LANES)
    share = frames.shape[1] // peers
    count = len(order)
    operands = [
        pltpu.with_memory_space_constraint(v, pltpu.HBM)
        for v in (frames, start_state, index, inlet_coupler)
    ]

    def kernel(*refs):
        inlet_kernel(order, *refs)

    return pl.pallas_call(
        kernel,
        in_specs=[pl.BlockSpec(memory_space=pltpu.HBM)] * len(operands),
        out_specs=[pl.BlockSpec(memory_space=pltpu.VMEM)] * count,
        out_shape=[pltpu.VMEM(out_shape, jnp.bfloat16)] * count,
        scratch_shapes=[
            pltpu.VMEM((count, share) + frames.shape[2:], frames.dtype),
            pltpu.VMEM((count, share) + start_state.shape[1:], start_state.dtype),
            pltpu.VMEM(index.shape, index.dtype),
            pltpu.VMEM(inlet_coupler.shape, inlet_coupler.dtype),
            pltpu.SemaphoreType.DMA((2, count + 1)),
        ],
        compiler_params=pltpu.CompilerParams(vmem_limit_bytes=VMEM_LIMIT),
    )(*operands)


def exchange(frames, start_state, tile_index, inlet_coupler, peers):
    order = partners(peers)
    got = []
    for part in (order[:2], order[2:-1], order[-1:]):
        packed = list(pack_for_peers(frames, start_state, tile_index, inlet_coupler, peers, part))
        tile_index, packed[0] = lax.optimization_barrier((tile_index, packed[0]))
        for k, block in zip(part, packed):
            if k:
                block = lax.ppermute(block, PLANE, [(p, p ^ k) for p in range(peers)])
            got.append(block)
    return got


def neighbour_choices(packed_ref, base, count_x, count_y, first_other):
    def entry(j, k):
        parts = []
        for i in range(count_x):
            rows = packed_ref[i * count_y + j, base:, :].astype(jnp.float32)
            parts.append(jnp.broadcast_to(rows[:, k : k + 1], (rows.shape[0], LANES)))
        return jnp.concatenate(parts, axis=0)

    columns = range(count_y)
    own = [entry(j, 0) for j in columns]
    torus_rows = own[0].shape[0]
    low = lax.broadcasted_iota(jnp.int32, own[0].shape, 0) % 2 == 0
    left = [entry(j, 3) for j in columns]
    right = [entry(j, 4) for j in columns]
    other = []
    for j in columns:
        other.append(
            [
                pltpu.roll(entry(j, 1), torus_rows - 2, axis=0),
                pltpu.roll(entry(j, 2), 2, axis=0),
                jnp.where(
                    low,
                    pltpu.roll(left[j], torus_rows - 1, axis=0),
                    pltpu.roll(left[(j + 1) % count_y], 1, axis=0),
                ),
                jnp.where(
                    low,
                    pltpu.roll(right[j - 1], torus_rows - 1, axis=0),
                    pltpu.roll(right[j], 1, axis=0),
                ),
            ]
        )

    def bits(choice):
        choice = choice.astype(jnp.int32)
        return [(choice >> bit) & 1 == 1 for bit in range(first_other.bit_length() - 1)]

    shares = [[(v == tile).astype(jnp.bfloat16) for tile in range(first_other)] for v in own]
    return shares, [[bits(v - first_other) for v in c] for c in other]


def steps_kernel(count_x, count_y, torus_rows, *refs):
    got_refs, (bank_ref, sent_ref, packed_ref) = refs[:-3], refs[-3:]
    peers, units = packed_ref.shape[0], bank_ref.shape[-1]
    place = place_in_plane()
    for k, got_ref in zip(partners(peers), got_refs):
        packed_ref[place ^ k] = got_ref[...]
    home_rows = torus_rows // count_x
    trajectories = sent_ref.shape[1] // home_rows
    drive_rows = trajectories * torus_rows
    state_rows = trajectories * home_rows
    halves = bank_ref.shape[0] // 2
    groups = [(j, t) for j in range(count_y) for t in range(trajectories)]

    def choose(index, products):
        chosen = []
        for piece in range(units // LANES):
            level = [product[:, piece * LANES : (piece + 1) * LANES] for product in products]
            for index_bit in index:
                level = [
                    jnp.where(index_bit, odd, even) for even, odd in zip(level[::2], level[1::2])
                ]
            chosen.append(level[0])
        return jnp.concatenate(chosen, axis=1)

    low = lax.broadcasted_iota(jnp.int32, (torus_rows, units), 0) % 2 == 0

    def share_of(rows, share):
        return rows.astype(jnp.bfloat16) * jnp.concatenate([share] * (units // LANES), axis=1)

    own_share, other_index = neighbour_choices(
        packed_ref, (drive_rows + state_rows) * units // LANES, count_x, count_y, halves
    )
    state = {}
    for j, t in groups:
        pieces = []
        for i in range(count_x):
            piece = load_rows(
                packed_ref, i * count_y + j, drive_rows * units // LANES, 0, state_rows, state_rows, units
            )
            pieces.append(piece.astype(jnp.float32)[t * home_rows : (t + 1) * home_rows])
        state[j, t] = jnp.concatenate(pieces, axis=0)
    parts = min(2, trajectories)
    for step in range(count_x):
        for part in range(parts):
            members = [(j, t) for j, t in groups if t % parts == part]
            state_half = jnp.concatenate([state[g].astype(jnp.bfloat16) for g in members], axis=0)
            masked = [
                jnp.concatenate([share_of(state[j, t], own_share[j][tile]) for j, t in members], axis=0)
                for tile in range(halves)
            ]
            own = jnp.dot(
                jnp.concatenate(masked, axis=1),
                bank_ref[:halves].reshape(halves * units, units),
                preferred_element_type=jnp.float32,
            )
            products = [
                jnp.dot(state_half, bank_ref[halves + tile], preferred_element_type=jnp.float32)
                for tile in range(halves)
            ]
            kept, left, right = {}, {}, {}
            for g, (j, t) in enumerate(members):
                span = slice(g * torus_rows, (g + 1) * torus_rows)
                others = [product[span] for product in products]
                total = own[span]
                total += pltpu.roll(choose(other_index[j][0], others), 2, axis=0)
                total += pltpu.roll(choose(other_index[j][1], others), torus_rows - 2, axis=0)
                kept[j, t] = total
                left[j, t] = choose(other_index[j][2], others)
                right[j, t] = choose(other_index[j][3], others)
            for j, t in members:
                before, behind = (j - 1) % count_y, (j + 1) % count_y
                crossing = jnp.where(
                    low, left[j, t] + right[behind, t], left[before, t] + right[j, t]
                )
                total = kept[j, t] + jnp.where(
                    low,
                    pltpu.roll(crossing, torus_rows - 1, axis=0),
                    pltpu.roll(crossing, 1, axis=0),
                )
                drive = load_rows(
                    packed_ref, step * count_y + j, 0, t * torus_rows, torus_rows, drive_rows, units
                )
                state[j, t] = jnp.tanh(total + drive.astype(jnp.float32))
    for i in range(count_x):
        for j in range(count_y):
            pieces = []
            for t in range(trajectories):
                pieces.append(state[j, t][i * home_rows : (i + 1) * home_rows])
            sent_ref[(i * count_y + j) ^ return_flip(peers)] = jnp.concatenate(pieces, axis=0).astype(jnp.bfloat16)


def run_steps(packed, tile_bank, count_x, count_y, torus_rows, home_rows):
    peers, units = len(packed), tile_bank.shape[-1]

    def kernel(*refs):
        steps_kernel(count_x, count_y, torus_rows, *refs)

    return pl.pallas_call(
        kernel,
        out_shape=jax.ShapeDtypeStruct((peers, home_rows, units), jnp.bfloat16),
        scratch_shapes=[pltpu.VMEM((peers,) + packed[0].shape, jnp.bfloat16)],
        compiler_params=pltpu.CompilerParams(vmem_limit_bytes=VMEM_LIMIT),
    )(*packed, tile_bank)


def readout_kernel(state_ref, readout_ref, field_ref, final_ref):
    units = state_ref.shape[-1]
    peers = state_ref.shape[0]
    half = jnp.concatenate([state_ref[p ^ return_flip(peers)] for p in range(peers)], axis=0)
    final = half.astype(jnp.float32)
    squares = (final * final).astype(jnp.bfloat16)
    field = jnp.dot(half, readout_ref[:units], preferred_element_type=jnp.float32)
    field += jnp.dot(squares, readout_ref[units:], preferred_element_type=jnp.float32)
    final_ref[...] = final.reshape(final_ref.shape)
    field_ref[...] = field.astype(jnp.bfloat16).reshape(field_ref.shape)


def read_out(state, readout_operator, block_shape):
    return pl.pallas_call(
        readout_kernel,
        out_shape=(
            jax.ShapeDtypeStruct(block_shape + readout_operator.shape[1:], jnp.bfloat16),
            jax.ShapeDtypeStruct(block_shape + state.shape[-1:], jnp.float32),
        ),
        compiler_params=pltpu.CompilerParams(vmem_limit_bytes=VMEM_LIMIT),
    )(state, readout_operator)


def by_trajectory(frames, start_state, tile_index, tile_bank, inlet_coupler, readout_operator):
    count_x, count_y = lax.axis_size("gx"), lax.axis_size("gy")
    peers = count_x * count_y
    units = inlet_coupler.shape[1]
    block_shape = start_state.shape[:-1]
    packed = exchange(frames, start_state, tile_index, inlet_coupler, peers)
    torus_rows = frames.shape[2] * frames.shape[3]
    home_rows = start_state.size // units // peers
    sent = run_steps(packed, tile_bank, count_x, count_y, torus_rows, home_rows)
    group = [p ^ return_flip(peers) for p in range(peers)]
    state = lax.all_to_all(sent, PLANE, 0, 0, tiled=True, axis_index_groups=[group])
    return read_out(state, readout_operator, block_shape)


def with_halo(cells, sides, width):
    for axis, dim in sides:
        count = lax.axis_size(axis)
        head = lax.slice_in_dim(cells, 0, width, axis=dim)
        tail = lax.slice_in_dim(cells, cells.shape[dim] - width, cells.shape[dim], axis=dim)
        cells = jnp.concatenate(
            [
                lax.ppermute(tail, axis, [(i, (i + 1) % count) for i in range(count)]),
                cells,
                lax.ppermute(head, axis, [((i + 1) % count, i) for i in range(count)]),
            ],
            axis=dim,
        )
    return cells


def by_block(frames, start_state, tile_index, tile_bank, inlet_coupler, readout_operator):
    patch_site_total = inlet_coupler.shape[0]
    hidden_node_total = inlet_coupler.shape[1]
    prediction_span = frames.shape[:-1]
    unrolled = jnp.dot(
        frames.reshape(-1, patch_site_total), inlet_coupler, preferred_element_type=jnp.float32
    )
    projected = unrolled.astype(jnp.bfloat16).reshape(prediction_span + (hidden_node_total,))
    input_signal = lax.all_to_all(projected, "gx", split_axis=2, concat_axis=0, tiled=True)
    chosen_tiles = tile_bank[tile_index]

    def advance(step_index, echo_system):
        state_half = echo_system.astype(jnp.bfloat16)
        extended = with_halo(state_half, (("gx", 1), ("gy", 2)), 1)
        adjacent_blocks = jnp.stack(
            [
                extended[:, 1:-1, 1:-1],
                extended[:, :-2, 1:-1],
                extended[:, 2:, 1:-1],
                extended[:, 1:-1, :-2],
                extended[:, 1:-1, 2:],
            ],
            axis=0,
        )
        coupled = jnp.einsum(
            "kcxyu,xykuv->cxyv", adjacent_blocks, chosen_tiles, preferred_element_type=jnp.float32
        )
        drive_now = lax.dynamic_index_in_dim(input_signal, step_index, 0, keepdims=False)
        return jnp.tanh(coupled + drive_now.astype(jnp.float32))

    echo_system = lax.fori_loop(0, input_signal.shape[0], advance, start_state)
    readout_basis = jnp.concatenate([echo_system, echo_system * echo_system], axis=-1).astype(
        jnp.bfloat16
    )
    prediction_span = readout_basis.shape[:-1]
    predicted_field = jnp.dot(
        readout_basis.reshape(-1, 2 * hidden_node_total),
        readout_operator,
        preferred_element_type=jnp.float32,
    )
    predicted_field = predicted_field.astype(jnp.bfloat16).reshape(
        prediction_span + (patch_site_total,)
    )
    return (predicted_field, echo_system)


def solution(mesh):
    placed = (
        P("gx", ("groups", "ta"), None, "gy", None),
        P(("groups", "ta"), "gx", "gy", None),
        P("gx", "gy", None),
        P(),
        P(),
        P(),
    )
    def shards(frames, start_state, tile_index, tile_bank, *rest):
        peers = mesh.shape["gx"] * mesh.shape["gy"]
        halves = tile_bank.shape[0] // 2
        fits = all(v & (v - 1) == 0 for v in (peers, halves))
        fits = fits and start_state.shape[0] % peers == 0 and start_state.shape[1] % 4 == 0
        fits = fits and start_state.shape[2] == 2 and start_state.shape[3] % LANES == 0
        body = by_trajectory if fits and frames.shape[0] == 1 else by_block
        return body(frames, start_state, tile_index, tile_bank, *rest)

    return jax.shard_map(
        shards,
        mesh=mesh,
        in_specs=placed,
        out_specs=(P(("groups", "ta"), "gx", "gy", None), P(("groups", "ta"), "gx", "gy", None)),
        check_vma=False,
    )
```

```python
import jax
import jax.numpy as jnp
from jax import lax
from jax.experimental import pallas as pl
from jax.experimental.pallas import tpu as pltpu
from jax.sharding import PartitionSpec as P

PLANE = ("gx", "gy")
LANES = 128
VMEM_LIMIT = 24 * 1024 * 1024


def whole(shape):
    return pl.BlockSpec(shape, lambda *_: (0,) * len(shape))


def place_in_plane():
    return lax.axis_index("gx") * lax.axis_size("gy") + lax.axis_index("gy")


def place_in_plane():
    return lax.axis_index("gx") * lax.axis_size("gy") + lax.axis_index("gy")


def partners(peers):
    served = (6, 7, 2, 5, 3, 4, 1)
    return sorted(range(1, peers), key=lambda k: served.index(k) if k in served else k) + [0]


def homeward(peers):
    listed = (5, 4, 1, 0, 7, 6, 3, 2)
    return sorted(range(peers), key=lambda place: listed.index(place) if place in listed else place)


def store_rows(ref, at, rows):
    for piece in range(rows.shape[1] // LANES):
        ref[at : at + rows.shape[0], :] = rows[:, piece * LANES : (piece + 1) * LANES]
        at += rows.shape[0]
    return at


def load_rows(ref, block, at, first, count, rows, units):
    pieces = []
    for piece in range(units // LANES):
        start = at + piece * rows + first
        pieces.append(ref[block, start : start + count, :])
    return jnp.concatenate(pieces, axis=1)


def inlet_kernel(order, frames_hbm, start_hbm, index_hbm, inlet_hbm, *refs):
    count = len(order)
    packed_refs, (frames_ref, start_ref, index_ref, inlet_ref, arrived) = refs[:count], refs[count:]
    units = inlet_ref.shape[1]
    place = place_in_plane()
    share = frames_ref.shape[1]
    entries = index_ref.shape[-1]
    cell_copies, state_copies = [], []
    for slot, k in enumerate(order):
        mine = pl.ds((place ^ k) * share, share)
        cell_copies.append(
            pltpu.make_async_copy(frames_hbm.at[0, mine], frames_ref.at[slot], arrived.at[0, slot])
        )
        state_copies.append(
            pltpu.make_async_copy(start_hbm.at[mine], start_ref.at[slot], arrived.at[1, slot])
        )
    inlet_copy = pltpu.make_async_copy(inlet_hbm, inlet_ref, arrived.at[0, count])
    index_copy = pltpu.make_async_copy(index_hbm, index_ref, arrived.at[1, count])
    inlet_copy.start()
    for copy in cell_copies:
        copy.start()
    index_copy.start()
    for copy in state_copies:
        copy.start()
    inlet_copy.wait()
    for slot, packed_ref in enumerate(packed_refs):
        cell_copies[slot].wait()
        cells = frames_ref[slot].reshape(-1, frames_ref.shape[-1])
        drive = jnp.dot(cells, inlet_ref[...], preferred_element_type=jnp.float32)
        after = store_rows(packed_ref, 0, drive.astype(jnp.bfloat16))
        if slot == 0:
            index_copy.wait()
            index = index_ref[...].astype(jnp.bfloat16)
            blank = jnp.zeros((index.shape[0], packed_ref.shape[1]), jnp.bfloat16)
        state_copies[slot].wait()
        state = start_ref[slot].reshape(-1, units)
        after = store_rows(packed_ref, after, state.astype(jnp.bfloat16))
        packed_ref[after:, :] = blank
        packed_ref[after:, :entries] = index


def pack_for_peers(frames, start_state, tile_index, inlet_coupler, peers, order):
    units = inlet_coupler.shape[1]
    blocks = tile_index.shape[0] * tile_index.shape[1]
    drive_rows = frames.size // frames.shape[-1] // peers
    state_rows = start_state.size // units // peers
    index = tile_index.reshape(blocks, -1)
    out_shape = ((drive_rows + state_rows) * units // LANES + blocks, LANES)
    share = frames.shape[1] // peers
    count = len(order)
    operands = [
        pltpu.with_memory_space_constraint(v, pltpu.HBM)
        for v in (frames, start_state, index, inlet_coupler)
    ]

    def kernel(*refs):
        inlet_kernel(order, *refs)

    return pl.pallas_call(
        kernel,
        in_specs=[pl.BlockSpec(memory_space=pltpu.HBM)] * len(operands),
        out_specs=[pl.BlockSpec(memory_space=pltpu.VMEM)] * count,
        out_shape=[pltpu.VMEM(out_shape, jnp.bfloat16)] * count,
        scratch_shapes=[
            pltpu.VMEM((count, share) + frames.shape[2:], frames.dtype),
            pltpu.VMEM((count, share) + start_state.shape[1:], start_state.dtype),
            pltpu.VMEM(index.shape, index.dtype),
            pltpu.VMEM(inlet_coupler.shape, inlet_coupler.dtype),
            pltpu.SemaphoreType.DMA((2, count + 1)),
        ],
        compiler_params=pltpu.CompilerParams(vmem_limit_bytes=VMEM_LIMIT),
    )(*operands)


def exchange(frames, start_state, tile_index, inlet_coupler, peers):
    order = partners(peers)
    got = []
    for part in (order[:2], order[2:-1], order[-1:]):
        packed = list(pack_for_peers(frames, start_state, tile_index, inlet_coupler, peers, part))
        tile_index, packed[0] = lax.optimization_barrier((tile_index, packed[0]))
        for k, block in zip(part, packed):
            if k:
                block = lax.ppermute(block, PLANE, [(p, p ^ k) for p in range(peers)])
            got.append(block)
    return got


def neighbour_choices(packed_ref, base, count_x, count_y, first_other):
    def entry(j, k):
        parts = []
        for i in range(count_x):
            rows = packed_ref[i * count_y + j, base:, :].astype(jnp.float32)
            parts.append(jnp.broadcast_to(rows[:, k : k + 1], (rows.shape[0], LANES)))
        return jnp.concatenate(parts, axis=0)

    columns = range(count_y)
    own = [entry(j, 0) for j in columns]
    torus_rows = own[0].shape[0]
    low = lax.broadcasted_iota(jnp.int32, own[0].shape, 0) % 2 == 0
    left = [entry(j, 3) for j in columns]
    right = [entry(j, 4) for j in columns]
    other = []
    for j in columns:
        other.append(
            [
                pltpu.roll(entry(j, 1), torus_rows - 2, axis=0),
                pltpu.roll(entry(j, 2), 2, axis=0),
                jnp.where(
                    low,
                    pltpu.roll(left[j], torus_rows - 1, axis=0),
                    pltpu.roll(left[(j + 1) % count_y], 1, axis=0),
                ),
                jnp.where(
                    low,
                    pltpu.roll(right[j - 1], torus_rows - 1, axis=0),
                    pltpu.roll(right[j], 1, axis=0),
                ),
            ]
        )

    def bits(choice):
        choice = choice.astype(jnp.int32)
        return [(choice >> bit) & 1 == 1 for bit in range(first_other.bit_length() - 1)]

    shares = [[(v == tile).astype(jnp.bfloat16) for tile in range(first_other)] for v in own]
    return shares, [[bits(v - first_other) for v in c] for c in other]


def steps_kernel(count_x, count_y, torus_rows, *refs):
    got_refs, (bank_ref, sent_ref, packed_ref) = refs[:-3], refs[-3:]
    peers, units = packed_ref.shape[0], bank_ref.shape[-1]
    place = place_in_plane()
    for k, got_ref in zip(partners(peers), got_refs):
        packed_ref[place ^ k] = got_ref[...]
    home_rows = torus_rows // count_x
    trajectories = sent_ref.shape[1] // home_rows
    drive_rows = trajectories * torus_rows
    state_rows = trajectories * home_rows
    halves = bank_ref.shape[0] // 2
    groups = [(j, t) for j in range(count_y) for t in range(trajectories)]

    def choose(index, products):
        chosen = []
        for piece in range(units // LANES):
            level = [product[:, piece * LANES : (piece + 1) * LANES] for product in products]
            for index_bit in index:
                level = [
                    jnp.where(index_bit, odd, even) for even, odd in zip(level[::2], level[1::2])
                ]
            chosen.append(level[0])
        return jnp.concatenate(chosen, axis=1)

    low = lax.broadcasted_iota(jnp.int32, (torus_rows, units), 0) % 2 == 0

    def share_of(rows, share):
        return rows.astype(jnp.bfloat16) * jnp.concatenate([share] * (units // LANES), axis=1)

    own_share, other_index = neighbour_choices(
        packed_ref, (drive_rows + state_rows) * units // LANES, count_x, count_y, halves
    )
    state = {}
    for j, t in groups:
        pieces = []
        for i in range(count_x):
            piece = load_rows(
                packed_ref, i * count_y + j, drive_rows * units // LANES, 0, state_rows, state_rows, units
            )
            pieces.append(piece.astype(jnp.float32)[t * home_rows : (t + 1) * home_rows])
        state[j, t] = jnp.concatenate(pieces, axis=0)
    parts = min(2, trajectories)
    for step in range(count_x):
        for part in range(parts):
            members = [(j, t) for j, t in groups if t % parts == part]
            state_half = jnp.concatenate([state[g].astype(jnp.bfloat16) for g in members], axis=0)
            products = [
                jnp.dot(state_half, bank_ref[halves + tile], preferred_element_type=jnp.float32)
                for tile in range(halves)
            ]
            masked = [
                jnp.concatenate([share_of(state[j, t], own_share[j][tile]) for j, t in members], axis=0)
                for tile in range(halves)
            ]
            own = jnp.dot(
                jnp.concatenate(masked, axis=1),
                bank_ref[:halves].reshape(halves * units, units),
                preferred_element_type=jnp.float32,
            )
            kept, left, right = {}, {}, {}
            for g, (j, t) in enumerate(members):
                span = slice(g * torus_rows, (g + 1) * torus_rows)
                others = [product[span] for product in products]
                total = own[span]
                total += pltpu.roll(choose(other_index[j][0], others), 2, axis=0)
                total += pltpu.roll(choose(other_index[j][1], others), torus_rows - 2, axis=0)
                kept[j, t] = total
                left[j, t] = choose(other_index[j][2], others)
                right[j, t] = choose(other_index[j][3], others)
            for j, t in members:
                before, behind = (j - 1) % count_y, (j + 1) % count_y
                crossing = jnp.where(
                    low, left[j, t] + right[behind, t], left[before, t] + right[j, t]
                )
                total = kept[j, t] + jnp.where(
                    low,
                    pltpu.roll(crossing, torus_rows - 1, axis=0),
                    pltpu.roll(crossing, 1, axis=0),
                )
                drive = load_rows(
                    packed_ref, step * count_y + j, 0, t * torus_rows, torus_rows, drive_rows, units
                )
                state[j, t] = jnp.tanh(total + drive.astype(jnp.float32))
    for i in range(count_x):
        for j in range(count_y):
            pieces = []
            for t in range(trajectories):
                pieces.append(state[j, t][i * home_rows : (i + 1) * home_rows])
            position = homeward(peers).index(i * count_y + j)
            sent_ref[position] = jnp.concatenate(pieces, axis=0).astype(jnp.bfloat16)


def run_steps(packed, tile_bank, count_x, count_y, torus_rows, home_rows):
    peers, units = len(packed), tile_bank.shape[-1]

    def kernel(*refs):
        steps_kernel(count_x, count_y, torus_rows, *refs)

    return pl.pallas_call(
        kernel,
        out_shape=jax.ShapeDtypeStruct((peers, home_rows, units), jnp.bfloat16),
        scratch_shapes=[pltpu.VMEM((peers,) + packed[0].shape, jnp.bfloat16)],
        compiler_params=pltpu.CompilerParams(vmem_limit_bytes=VMEM_LIMIT),
    )(*packed, tile_bank)


def readout_kernel(state_ref, readout_ref, field_ref, final_ref):
    units = state_ref.shape[-1]
    peers = state_ref.shape[0]
    half = jnp.concatenate(
        [state_ref[homeward(peers).index(place)] for place in range(peers)], axis=0
    )
    final = half.astype(jnp.float32)
    squares = (final * final).astype(jnp.bfloat16)
    field = jnp.dot(half, readout_ref[:units], preferred_element_type=jnp.float32)
    field += jnp.dot(squares, readout_ref[units:], preferred_element_type=jnp.float32)
    final_ref[...] = final.reshape(final_ref.shape)
    field_ref[...] = field.astype(jnp.bfloat16).reshape(field_ref.shape)


def read_out(state, readout_operator, block_shape):
    return pl.pallas_call(
        readout_kernel,
        out_shape=(
            jax.ShapeDtypeStruct(block_shape + readout_operator.shape[1:], jnp.bfloat16),
            jax.ShapeDtypeStruct(block_shape + state.shape[-1:], jnp.float32),
        ),
        compiler_params=pltpu.CompilerParams(vmem_limit_bytes=VMEM_LIMIT),
    )(state, readout_operator)


def by_trajectory(frames, start_state, tile_index, tile_bank, inlet_coupler, readout_operator):
    count_x, count_y = lax.axis_size("gx"), lax.axis_size("gy")
    peers = count_x * count_y
    units = inlet_coupler.shape[1]
    block_shape = start_state.shape[:-1]
    packed = exchange(frames, start_state, tile_index, inlet_coupler, peers)
    torus_rows = frames.shape[2] * frames.shape[3]
    home_rows = start_state.size // units // peers
    sent = run_steps(packed, tile_bank, count_x, count_y, torus_rows, home_rows)
    state = lax.all_to_all(sent, PLANE, 0, 0, tiled=True, axis_index_groups=[homeward(peers)])
    return read_out(state, readout_operator, block_shape)


def with_halo(cells, sides, width):
    for axis, dim in sides:
        count = lax.axis_size(axis)
        head = lax.slice_in_dim(cells, 0, width, axis=dim)
        tail = lax.slice_in_dim(cells, cells.shape[dim] - width, cells.shape[dim], axis=dim)
        cells = jnp.concatenate(
            [
                lax.ppermute(tail, axis, [(i, (i + 1) % count) for i in range(count)]),
                cells,
                lax.ppermute(head, axis, [((i + 1) % count, i) for i in range(count)]),
            ],
            axis=dim,
        )
    return cells


def by_block(frames, start_state, tile_index, tile_bank, inlet_coupler, readout_operator):
    patch_site_total = inlet_coupler.shape[0]
    hidden_node_total = inlet_coupler.shape[1]
    prediction_span = frames.shape[:-1]
    unrolled = jnp.dot(
        frames.reshape(-1, patch_site_total), inlet_coupler, preferred_element_type=jnp.float32
    )
    projected = unrolled.astype(jnp.bfloat16).reshape(prediction_span + (hidden_node_total,))
    input_signal = lax.all_to_all(projected, "gx", split_axis=2, concat_axis=0, tiled=True)
    chosen_tiles = tile_bank[tile_index]

    def advance(step_index, echo_system):
        state_half = echo_system.astype(jnp.bfloat16)
        extended = with_halo(state_half, (("gx", 1), ("gy", 2)), 1)
        adjacent_blocks = jnp.stack(
            [
                extended[:, 1:-1, 1:-1],
                extended[:, :-2, 1:-1],
                extended[:, 2:, 1:-1],
                extended[:, 1:-1, :-2],
                extended[:, 1:-1, 2:],
            ],
            axis=0,
        )
        coupled = jnp.einsum(
            "kcxyu,xykuv->cxyv", adjacent_blocks, chosen_tiles, preferred_element_type=jnp.float32
        )
        drive_now = lax.dynamic_index_in_dim(input_signal, step_index, 0, keepdims=False)
        return jnp.tanh(coupled + drive_now.astype(jnp.float32))

    echo_system = lax.fori_loop(0, input_signal.shape[0], advance, start_state)
    readout_basis = jnp.concatenate([echo_system, echo_system * echo_system], axis=-1).astype(
        jnp.bfloat16
    )
    prediction_span = readout_basis.shape[:-1]
    predicted_field = jnp.dot(
        readout_basis.reshape(-1, 2 * hidden_node_total),
        readout_operator,
        preferred_element_type=jnp.float32,
    )
    predicted_field = predicted_field.astype(jnp.bfloat16).reshape(
        prediction_span + (patch_site_total,)
    )
    return (predicted_field, echo_system)


def solution(mesh):
    placed = (
        P("gx", ("groups", "ta"), None, "gy", None),
        P(("groups", "ta"), "gx", "gy", None),
        P("gx", "gy", None),
        P(),
        P(),
        P(),
    )
    def shards(frames, start_state, tile_index, tile_bank, *rest):
        peers = mesh.shape["gx"] * mesh.shape["gy"]
        halves = tile_bank.shape[0] // 2
        fits = all(v & (v - 1) == 0 for v in (peers, halves))
        fits = fits and start_state.shape[0] % peers == 0 and start_state.shape[1] % 4 == 0
        fits = fits and start_state.shape[2] == 2 and start_state.shape[3] % LANES == 0
        body = by_trajectory if fits and frames.shape[0] == 1 else by_block
        return body(frames, start_state, tile_index, tile_bank, *rest)

    return jax.shard_map(
        shards,
        mesh=mesh,
        in_specs=placed,
        out_specs=(P(("groups", "ta"), "gx", "gy", None), P(("groups", "ta"), "gx", "gy", None)),
        check_vma=False,
    )
```

```python
import jax
import jax.numpy as jnp
from jax import lax
from jax.experimental import pallas as pl
from jax.experimental.pallas import tpu as pltpu
from jax.sharding import PartitionSpec as P

PLANE = ("gx", "gy")
LANES = 128
VMEM_LIMIT = 24 * 1024 * 1024


def whole(shape):
    return pl.BlockSpec(shape, lambda *_: (0,) * len(shape))


def place_in_plane():
    return lax.axis_index("gx") * lax.axis_size("gy") + lax.axis_index("gy")


def place_in_plane():
    return lax.axis_index("gx") * lax.axis_size("gy") + lax.axis_index("gy")


def partners(peers):
    served = (6, 7, 2, 5, 3, 4, 1)
    return sorted(range(1, peers), key=lambda k: served.index(k) if k in served else k) + [0]


def homeward(peers):
    listed = (5, 4, 1, 0, 7, 6, 3, 2)
    return sorted(range(peers), key=lambda place: listed.index(place) if place in listed else place)


def store_rows(ref, at, rows):
    for piece in range(rows.shape[1] // LANES):
        ref[at : at + rows.shape[0], :] = rows[:, piece * LANES : (piece + 1) * LANES]
        at += rows.shape[0]
    return at


def load_rows(ref, block, at, first, count, rows, units):
    pieces = []
    for piece in range(units // LANES):
        start = at + piece * rows + first
        pieces.append(ref[block, start : start + count, :])
    return jnp.concatenate(pieces, axis=1)


def inlet_kernel(order, frames_hbm, start_hbm, index_hbm, inlet_hbm, *refs):
    count = len(order)
    packed_refs, (frames_ref, start_ref, index_ref, inlet_ref, arrived) = refs[:count], refs[count:]
    units = inlet_ref.shape[1]
    place = place_in_plane()
    share = frames_ref.shape[1]
    entries = index_ref.shape[-1]
    cell_copies, state_copies = [], []
    for slot, k in enumerate(order):
        mine = pl.ds((place ^ k) * share, share)
        cell_copies.append(
            pltpu.make_async_copy(frames_hbm.at[0, mine], frames_ref.at[slot], arrived.at[0, slot])
        )
        state_copies.append(
            pltpu.make_async_copy(start_hbm.at[mine], start_ref.at[slot], arrived.at[1, slot])
        )
    inlet_copy = pltpu.make_async_copy(inlet_hbm, inlet_ref, arrived.at[0, count])
    index_copy = pltpu.make_async_copy(index_hbm, index_ref, arrived.at[1, count])
    inlet_copy.start()
    for copy in cell_copies:
        copy.start()
    index_copy.start()
    for copy in state_copies:
        copy.start()
    inlet_copy.wait()
    for slot, packed_ref in enumerate(packed_refs):
        cell_copies[slot].wait()
        cells = frames_ref[slot].reshape(-1, frames_ref.shape[-1])
        drive = jnp.dot(cells, inlet_ref[...], preferred_element_type=jnp.float32)
        after = store_rows(packed_ref, 0, drive.astype(jnp.bfloat16))
        if slot == 0:
            index_copy.wait()
            index = index_ref[...].astype(jnp.bfloat16)
            blank = jnp.zeros((index.shape[0], packed_ref.shape[1]), jnp.bfloat16)
        state_copies[slot].wait()
        state = start_ref[slot].reshape(-1, units)
        after = store_rows(packed_ref, after, state.astype(jnp.bfloat16))
        packed_ref[after:, :] = blank
        packed_ref[after:, :entries] = index


def pack_for_peers(frames, start_state, tile_index, inlet_coupler, peers, order):
    units = inlet_coupler.shape[1]
    blocks = tile_index.shape[0] * tile_index.shape[1]
    drive_rows = frames.size // frames.shape[-1] // peers
    state_rows = start_state.size // units // peers
    index = tile_index.reshape(blocks, -1)
    out_shape = ((drive_rows + state_rows) * units // LANES + blocks, LANES)
    share = frames.shape[1] // peers
    count = len(order)
    operands = [
        pltpu.with_memory_space_constraint(v, pltpu.HBM)
        for v in (frames, start_state, index, inlet_coupler)
    ]

    def kernel(*refs):
        inlet_kernel(order, *refs)

    return pl.pallas_call(
        kernel,
        in_specs=[pl.BlockSpec(memory_space=pltpu.HBM)] * len(operands),
        out_specs=[pl.BlockSpec(memory_space=pltpu.VMEM)] * count,
        out_shape=[pltpu.VMEM(out_shape, jnp.bfloat16)] * count,
        scratch_shapes=[
            pltpu.VMEM((count, share) + frames.shape[2:], frames.dtype),
            pltpu.VMEM((count, share) + start_state.shape[1:], start_state.dtype),
            pltpu.VMEM(index.shape, index.dtype),
            pltpu.VMEM(inlet_coupler.shape, inlet_coupler.dtype),
            pltpu.SemaphoreType.DMA((2, count + 1)),
        ],
        compiler_params=pltpu.CompilerParams(vmem_limit_bytes=VMEM_LIMIT),
    )(*operands)


def exchange(frames, start_state, tile_index, inlet_coupler, peers):
    order = partners(peers)
    got = []
    for part in (order[:3], order[3:-1], order[-1:]):
        packed = list(pack_for_peers(frames, start_state, tile_index, inlet_coupler, peers, part))
        tile_index, packed[0] = lax.optimization_barrier((tile_index, packed[0]))
        for k, block in zip(part, packed):
            if k:
                block = lax.ppermute(block, PLANE, [(p, p ^ k) for p in range(peers)])
            got.append(block)
    return got


def neighbour_choices(packed_ref, base, count_x, count_y, first_other):
    def entry(j, k):
        parts = []
        for i in range(count_x):
            rows = packed_ref[i * count_y + j, base:, :].astype(jnp.float32)
            parts.append(jnp.broadcast_to(rows[:, k : k + 1], (rows.shape[0], LANES)))
        return jnp.concatenate(parts, axis=0)

    columns = range(count_y)
    own = [entry(j, 0) for j in columns]
    torus_rows = own[0].shape[0]
    low = lax.broadcasted_iota(jnp.int32, own[0].shape, 0) % 2 == 0
    left = [entry(j, 3) for j in columns]
    right = [entry(j, 4) for j in columns]
    other = []
    for j in columns:
        other.append(
            [
                pltpu.roll(entry(j, 1), torus_rows - 2, axis=0),
                pltpu.roll(entry(j, 2), 2, axis=0),
                jnp.where(
                    low,
                    pltpu.roll(left[j], torus_rows - 1, axis=0),
                    pltpu.roll(left[(j + 1) % count_y], 1, axis=0),
                ),
                jnp.where(
                    low,
                    pltpu.roll(right[j - 1], torus_rows - 1, axis=0),
                    pltpu.roll(right[j], 1, axis=0),
                ),
            ]
        )

    def bits(choice):
        choice = choice.astype(jnp.int32)
        return [(choice >> bit) & 1 == 1 for bit in range(first_other.bit_length() - 1)]

    shares = [[(v == tile).astype(jnp.bfloat16) for tile in range(first_other)] for v in own]
    return shares, [[bits(v - first_other) for v in c] for c in other]


def steps_kernel(count_x, count_y, torus_rows, *refs):
    got_refs, (bank_ref, sent_ref, packed_ref) = refs[:-3], refs[-3:]
    peers, units = packed_ref.shape[0], bank_ref.shape[-1]
    place = place_in_plane()
    for k, got_ref in zip(partners(peers), got_refs):
        packed_ref[place ^ k] = got_ref[...]
    home_rows = torus_rows // count_x
    trajectories = sent_ref.shape[1] // home_rows
    drive_rows = trajectories * torus_rows
    state_rows = trajectories * home_rows
    halves = bank_ref.shape[0] // 2
    groups = [(j, t) for j in range(count_y) for t in range(trajectories)]

    def choose(index, products):
        chosen = []
        for piece in range(units // LANES):
            level = [product[:, piece * LANES : (piece + 1) * LANES] for product in products]
            for index_bit in index:
                level = [
                    jnp.where(index_bit, odd, even) for even, odd in zip(level[::2], level[1::2])
                ]
            chosen.append(level[0])
        return jnp.concatenate(chosen, axis=1)

    low = lax.broadcasted_iota(jnp.int32, (torus_rows, units), 0) % 2 == 0

    def share_of(rows, share):
        return rows.astype(jnp.bfloat16) * jnp.concatenate([share] * (units // LANES), axis=1)

    own_share, other_index = neighbour_choices(
        packed_ref, (drive_rows + state_rows) * units // LANES, count_x, count_y, halves
    )
    state = {}
    for j, t in groups:
        pieces = []
        for i in range(count_x):
            piece = load_rows(
                packed_ref, i * count_y + j, drive_rows * units // LANES, 0, state_rows, state_rows, units
            )
            pieces.append(piece.astype(jnp.float32)[t * home_rows : (t + 1) * home_rows])
        state[j, t] = jnp.concatenate(pieces, axis=0)
    parts = min(2, trajectories)
    for step in range(count_x):
        for part in range(parts):
            members = [(j, t) for j, t in groups if t % parts == part]
            state_half = jnp.concatenate([state[g].astype(jnp.bfloat16) for g in members], axis=0)
            products = [
                jnp.dot(state_half, bank_ref[halves + tile], preferred_element_type=jnp.float32)
                for tile in range(halves)
            ]
            masked = [
                jnp.concatenate([share_of(state[j, t], own_share[j][tile]) for j, t in members], axis=0)
                for tile in range(halves)
            ]
            own = sum(
                jnp.dot(rows, bank_ref[tile], preferred_element_type=jnp.float32)
                for tile, rows in enumerate(masked)
            )
            kept, left, right = {}, {}, {}
            for g, (j, t) in enumerate(members):
                span = slice(g * torus_rows, (g + 1) * torus_rows)
                others = [product[span] for product in products]
                total = own[span]
                total += pltpu.roll(choose(other_index[j][0], others), 2, axis=0)
                total += pltpu.roll(choose(other_index[j][1], others), torus_rows - 2, axis=0)
                kept[j, t] = total
                left[j, t] = choose(other_index[j][2], others)
                right[j, t] = choose(other_index[j][3], others)
            for j, t in members:
                before, behind = (j - 1) % count_y, (j + 1) % count_y
                crossing = jnp.where(
                    low, left[j, t] + right[behind, t], left[before, t] + right[j, t]
                )
                total = kept[j, t] + jnp.where(
                    low,
                    pltpu.roll(crossing, torus_rows - 1, axis=0),
                    pltpu.roll(crossing, 1, axis=0),
                )
                drive = load_rows(
                    packed_ref, step * count_y + j, 0, t * torus_rows, torus_rows, drive_rows, units
                )
                state[j, t] = jnp.tanh(total + drive.astype(jnp.float32))
    for i in range(count_x):
        for j in range(count_y):
            pieces = []
            for t in range(trajectories):
                pieces.append(state[j, t][i * home_rows : (i + 1) * home_rows])
            position = homeward(peers).index(i * count_y + j)
            sent_ref[position] = jnp.concatenate(pieces, axis=0).astype(jnp.bfloat16)


def run_steps(packed, tile_bank, count_x, count_y, torus_rows, home_rows):
    peers, units = len(packed), tile_bank.shape[-1]

    def kernel(*refs):
        steps_kernel(count_x, count_y, torus_rows, *refs)

    return pl.pallas_call(
        kernel,
        out_shape=jax.ShapeDtypeStruct((peers, home_rows, units), jnp.bfloat16),
        scratch_shapes=[pltpu.VMEM((peers,) + packed[0].shape, jnp.bfloat16)],
        compiler_params=pltpu.CompilerParams(vmem_limit_bytes=VMEM_LIMIT),
    )(*packed, tile_bank)


def readout_kernel(state_ref, readout_ref, field_ref, final_ref):
    units = state_ref.shape[-1]
    peers = state_ref.shape[0]
    half = jnp.concatenate(
        [state_ref[homeward(peers).index(place)] for place in range(peers)], axis=0
    )
    final = half.astype(jnp.float32)
    squares = (final * final).astype(jnp.bfloat16)
    field = jnp.dot(half, readout_ref[:units], preferred_element_type=jnp.float32)
    field += jnp.dot(squares, readout_ref[units:], preferred_element_type=jnp.float32)
    final_ref[...] = final.reshape(final_ref.shape)
    field_ref[...] = field.astype(jnp.bfloat16).reshape(field_ref.shape)


def read_out(state, readout_operator, block_shape):
    return pl.pallas_call(
        readout_kernel,
        out_shape=(
            jax.ShapeDtypeStruct(block_shape + readout_operator.shape[1:], jnp.bfloat16),
            jax.ShapeDtypeStruct(block_shape + state.shape[-1:], jnp.float32),
        ),
        compiler_params=pltpu.CompilerParams(vmem_limit_bytes=VMEM_LIMIT),
    )(state, readout_operator)


def by_trajectory(frames, start_state, tile_index, tile_bank, inlet_coupler, readout_operator):
    count_x, count_y = lax.axis_size("gx"), lax.axis_size("gy")
    peers = count_x * count_y
    units = inlet_coupler.shape[1]
    block_shape = start_state.shape[:-1]
    packed = exchange(frames, start_state, tile_index, inlet_coupler, peers)
    torus_rows = frames.shape[2] * frames.shape[3]
    home_rows = start_state.size // units // peers
    sent = run_steps(packed, tile_bank, count_x, count_y, torus_rows, home_rows)
    state = lax.all_to_all(sent, PLANE, 0, 0, tiled=True, axis_index_groups=[homeward(peers)])
    return read_out(state, readout_operator, block_shape)


def with_halo(cells, sides, width):
    for axis, dim in sides:
        count = lax.axis_size(axis)
        head = lax.slice_in_dim(cells, 0, width, axis=dim)
        tail = lax.slice_in_dim(cells, cells.shape[dim] - width, cells.shape[dim], axis=dim)
        cells = jnp.concatenate(
            [
                lax.ppermute(tail, axis, [(i, (i + 1) % count) for i in range(count)]),
                cells,
                lax.ppermute(head, axis, [((i + 1) % count, i) for i in range(count)]),
            ],
            axis=dim,
        )
    return cells


def by_block(frames, start_state, tile_index, tile_bank, inlet_coupler, readout_operator):
    patch_site_total = inlet_coupler.shape[0]
    hidden_node_total = inlet_coupler.shape[1]
    prediction_span = frames.shape[:-1]
    unrolled = jnp.dot(
        frames.reshape(-1, patch_site_total), inlet_coupler, preferred_element_type=jnp.float32
    )
    projected = unrolled.astype(jnp.bfloat16).reshape(prediction_span + (hidden_node_total,))
    input_signal = lax.all_to_all(projected, "gx", split_axis=2, concat_axis=0, tiled=True)
    chosen_tiles = tile_bank[tile_index]

    def advance(step_index, echo_system):
        state_half = echo_system.astype(jnp.bfloat16)
        extended = with_halo(state_half, (("gx", 1), ("gy", 2)), 1)
        adjacent_blocks = jnp.stack(
            [
                extended[:, 1:-1, 1:-1],
                extended[:, :-2, 1:-1],
                extended[:, 2:, 1:-1],
                extended[:, 1:-1, :-2],
                extended[:, 1:-1, 2:],
            ],
            axis=0,
        )
        coupled = jnp.einsum(
            "kcxyu,xykuv->cxyv", adjacent_blocks, chosen_tiles, preferred_element_type=jnp.float32
        )
        drive_now = lax.dynamic_index_in_dim(input_signal, step_index, 0, keepdims=False)
        return jnp.tanh(coupled + drive_now.astype(jnp.float32))

    echo_system = lax.fori_loop(0, input_signal.shape[0], advance, start_state)
    readout_basis = jnp.concatenate([echo_system, echo_system * echo_system], axis=-1).astype(
        jnp.bfloat16
    )
    prediction_span = readout_basis.shape[:-1]
    predicted_field = jnp.dot(
        readout_basis.reshape(-1, 2 * hidden_node_total),
        readout_operator,
        preferred_element_type=jnp.float32,
    )
    predicted_field = predicted_field.astype(jnp.bfloat16).reshape(
        prediction_span + (patch_site_total,)
    )
    return (predicted_field, echo_system)


def solution(mesh):
    placed = (
        P("gx", ("groups", "ta"), None, "gy", None),
        P(("groups", "ta"), "gx", "gy", None),
        P("gx", "gy", None),
        P(),
        P(),
        P(),
    )
    def shards(frames, start_state, tile_index, tile_bank, *rest):
        peers = mesh.shape["gx"] * mesh.shape["gy"]
        halves = tile_bank.shape[0] // 2
        fits = all(v & (v - 1) == 0 for v in (peers, halves))
        fits = fits and start_state.shape[0] % peers == 0 and start_state.shape[1] % 4 == 0
        fits = fits and start_state.shape[2] == 2 and start_state.shape[3] % LANES == 0
        body = by_trajectory if fits and frames.shape[0] == 1 else by_block
        return body(frames, start_state, tile_index, tile_bank, *rest)

    return jax.shard_map(
        shards,
        mesh=mesh,
        in_specs=placed,
        out_specs=(P(("groups", "ta"), "gx", "gy", None), P(("groups", "ta"), "gx", "gy", None)),
        check_vma=False,
    )
```
